32 devices in a mesh: shot: 8 (over z, y), gx: 4 (over x, core).
Axes of the slice: x: 2, y: 2, z: 4, core: 2. Of those that a mesh axis runs over, the one named last changes fastest.
Arguments:
- source_prev: float32 [8, 64, 64, 128], P('shot', 'gx'), may hold values from -6 to 6
- source_now: float32 [8, 64, 64, 128], P('shot', 'gx'), may hold values from -6 to 6
- receiver_prev: float32 [8, 64, 64, 128], P('shot', 'gx'), may hold values from -6 to 6
- receiver_now: float32 [8, 64, 64, 128], P('shot', 'gx'), may hold values from -6 to 6
- courant: float32 [64, 64, 128], P('gx'), may hold values from 0.05 to 0.3
- source_cells: int32 [8, 8], P('shot'), may hold values from 0 to 524287
- wavelet: float32 [8, 2, 8], P('shot'), may hold values from -128 to 128
- receiver_cells: int32 [8, 512], P('shot'), may hold values from 0 to 524287
- receiver_data: float32 [8, 2, 512], P('shot'), may hold values from -128 to 128
- offsets: int32 [9], replicated, may hold values from -8 to 8, as said below
- conv_weight: float32 [64, 9, 3, 3, 3], replicated, may hold values from -1.25 to 1.25
- conv_bias: float32 [64], replicated, may hold values from -3 to 3
Outputs:
- summary: float32 [64, 16, 512], P(None, 'gx', 'shot')
The draws below stay inside these ranges and needn't reach their ends.
Inputs may be any that keep to these rules, and one draw needn't show every extreme that they name: The offsets are distinct and include -8 and 8.
All inputs are finite; a program needn't handle non-finite values.
Results may differ from the reference program's by a relative error of at most 0.0003.
Values sent between devices are 32-bit elements; how exact they have to be, the bound alone decides.
A program may use at most 64 MiB of HBM per device.

```python
import jax
import jax.numpy as jnp
from jax import lax

NY = 64
NZ = 128
HMAX = 8
OFFS = 9
OUT_CH = 64
SHOTS = 8
RECS = 512
GROUPS = 8
NX = 64


def draw_offsets(key, part):
    inner = jnp.arange(-HMAX + 1, HMAX, dtype=jnp.int32)
    picked = jax.random.permutation(key, inner)[:OFFS - 2]
    return jnp.concatenate([jnp.array([-HMAX, HMAX], jnp.int32), picked]).astype(jnp.int32)


def set_ends(entries, stream_key, smallest, largest):
    place = [jax.random.randint(jax.random.fold_in(stream_key, axis), (), 0, length) for axis, length in enumerate(entries.shape)]
    widest = entries.shape.index(max(entries.shape))
    beside = place[:widest] + [(place[widest] + 1) % entries.shape[widest]] + place[widest + 1:]
    return entries.at[tuple(place)].set(smallest).at[tuple(beside)].set(largest)


def steps_of(rng, shape, split, least, high):
    def one(dim, parts):
        heights = jax.random.uniform(jax.random.fold_in(jax.random.fold_in(rng, 6), dim), (parts,), jnp.float32, least / len(split), high / len(split))
        return jnp.repeat(jnp.exp(heights), shape[dim] // parts).reshape((-1,) + (1,) * (len(shape) - dim - 1))

    level = one(*split[0])
    for cut in split[1:]:
        level = level * one(*cut)
    return level


def centred(rng, dims, spread, bound, pieces=(), kind=jnp.bfloat16):
    values = jax.random.normal(rng, dims, jnp.float32) * spread
    if len(pieces) > 0:
        values = steps_of(rng, dims, pieces, -0.22, 0.18) * values
    return jnp.clip(values, min=-bound, max=bound).astype(kind)


def setup_inputs(seed: int = 0) -> dict:
    key_of = jax.random.split(jax.random.key(seed), 13)
    return {
        "source_prev": centred(key_of[0], (GROUPS, NX, NY, NZ), 1.0, 6.0, ((0, 8), (1, 4)), jnp.float32),
        "source_now": centred(key_of[1], (GROUPS, NX, NY, NZ), 1.0, 6.0, ((0, 8), (1, 4)), jnp.float32),
        "receiver_prev": centred(key_of[2], (GROUPS, NX, NY, NZ), 1.0, 6.0, ((0, 8), (1, 4)), jnp.float32),
        "receiver_now": centred(key_of[3], (GROUPS, NX, NY, NZ), 1.0, 6.0, ((0, 8), (1, 4)), jnp.float32),
        "courant": jnp.clip(0.05 + 0.25 * jax.random.uniform(key_of[4], (NX, NY, NZ), jnp.float32) ** steps_of(key_of[4], (NX, NY, NZ), ((0, 4),), -0.2, 0.2), 0.05, 0.3),
        "source_cells": set_ends(jax.random.randint(key_of[5], (GROUPS, SHOTS), 0, NX * NY * NZ), jax.random.fold_in(key_of[5], 1), 0, (NX * NY * NZ) - 1).astype(jnp.int32),
        "wavelet": centred(key_of[6], (GROUPS, 2, SHOTS), 20.0, 128.0, ((0, 8),), jnp.float32),
        "receiver_cells": set_ends(jax.random.randint(key_of[7], (GROUPS, RECS), 0, NX * NY * NZ), jax.random.fold_in(key_of[7], 1), 0, (NX * NY * NZ) - 1).astype(jnp.int32),
        "receiver_data": centred(key_of[8], (GROUPS, 2, RECS), 20.0, 128.0, ((0, 8),), jnp.float32),
        "offsets": draw_offsets(jax.random.fold_in(key_of[12], 71), 0),
        "conv_weight": centred(key_of[10], (OUT_CH, OFFS, 3, 3, 3), 27 ** -0.5, 1.25, (), jnp.float32),
        "conv_bias": centred(key_of[11], (OUT_CH,), 0.5, 3.0, (), jnp.float32),
    }


def inject(cells_here, first_x, cell_index, amplitudes, size_y, size_z):
    plane_size = size_y * size_z
    column = cell_index // plane_size
    within = cell_index % plane_size
    local_x = column - first_x
    inside = (local_x >= 0) & (local_x < cells_here)
    target = jnp.where(inside, local_x * plane_size + within, cells_here * plane_size).astype(jnp.int32)
    flat_cells = jnp.zeros((cells_here * plane_size + 1,), jnp.float32).at[target].add(amplitudes.astype(jnp.float32))
    return flat_cells[:-1].reshape(cells_here, size_y, size_z)


def laplace_step(previous, extended, courant, sources):
    center = extended[:, 1:-1]
    padded = jnp.pad(center, ((0, 0), (0, 0), (1, 1), (1, 1)))
    laplace = extended[:, 2:] + extended[:, :-2]
    laplace = laplace + padded[:, :, 2:, 1:-1] + padded[:, :, :-2, 1:-1]
    laplace = laplace + padded[:, :, 1:-1, 2:] + padded[:, :, 1:-1, :-2] - 6.0 * center
    return 2.0 * center - previous + courant * laplace + sources


def coarsen(image_block):
    size_x, size_y, size_z = image_block.shape
    return image_block.reshape(size_x // 4, 4, size_y // 4, 4, size_z // 4, 4).mean(axis=(1, 3, 5))


def offset_image(wide, offsets, margin, cells_x):
    def per_offset(offset_value):
        forward_part = lax.dynamic_slice_in_dim(wide, (margin + offset_value).astype(jnp.int32), cells_x, 1)
        backward_part = lax.dynamic_slice_in_dim(wide, (margin - offset_value).astype(jnp.int32), cells_x, 1)
        image_block = forward_part[0] * backward_part[1] + forward_part[2] * backward_part[3]
        return coarsen(image_block)
    return lax.map(per_offset, offsets)


def conv_apply(padded, conv_weight, conv_bias):
    channels, span_x, span_y, span_z = padded.shape
    size_x, size_y, size_z = span_x - 2, span_y - 2, span_z - 2
    patches = jnp.stack([padded[:, step_x:step_x + size_x, step_y:step_y + size_y, step_z:step_z + size_z]
                         for step_x in range(3) for step_y in range(3) for step_z in range(3)], axis=1)
    patches = patches.reshape(channels * 27, size_x * size_y * size_z)
    matrix = conv_weight.reshape(conv_weight.shape[0], channels * 27)
    result = jnp.dot(matrix, patches, precision=lax.Precision.HIGHEST, preferred_element_type=jnp.float32)
    result = result + conv_bias[:, None]
    return result.reshape(conv_weight.shape[0], size_x, size_y * size_z)


def reference(source_prev, source_now, receiver_prev, receiver_now, courant, source_cells, wavelet, receiver_cells, receiver_data, offsets, conv_weight, conv_bias):
    grid_x, size_y, size_z = courant.shape

    def per_group(packed):
        s_prev, s_now, r_prev, r_now, s_cells, s_amp, r_cells, r_amp = packed
        previous = jnp.stack([s_prev, r_prev])
        current = jnp.stack([s_now, r_now])
        levels = []
        for step_index in range(2):
            extended = jnp.pad(current, ((0, 0), (1, 1), (0, 0), (0, 0)))
            sources = jnp.stack([inject(grid_x, 0, s_cells, s_amp[step_index], size_y, size_z),
                                 inject(grid_x, 0, r_cells, r_amp[step_index], size_y, size_z)])
            advanced = laplace_step(previous, extended, courant, sources)
            previous, current = current, advanced
            levels.append(advanced)
        fields = jnp.concatenate(levels, axis=0)
        wide = jnp.pad(fields, ((0, 0), (HMAX, HMAX), (0, 0), (0, 0)))
        return offset_image(wide, offsets, HMAX, grid_x)

    coarse = lax.map(per_group, (source_prev, source_now, receiver_prev, receiver_now,
                                 source_cells, wavelet, receiver_cells, receiver_data))
    summed = jnp.sum(coarse, axis=0)
    padded = jnp.pad(summed, ((0, 0), (1, 1), (1, 1), (1, 1)))
    return conv_apply(padded, conv_weight, conv_bias)
```

```python
import functools

import jax
import jax.numpy as jnp
from jax import lax
from jax.experimental import pallas as pl
from jax.experimental.pallas import tpu as pltpu
from jax.sharding import PartitionSpec as P

HMAX = 8
MESH = pl.DeviceIdType.MESH


def kernel(
    dims,
    sp_ref,
    sn_ref,
    rp_ref,
    rn_ref,
    courant_ref,
    scells_ref,
    wavelet_ref,
    rcells_ref,
    rdata_ref,
    offsets_ref,
    weight_ref,
    out_ref,
    now,
    prev,
    cour,
    first_lev,
    second_lev,
    inj,
    acc,
    pads,
    padi,
    rows,
    parts,
    summed,
    patches,
    load_sem,
    edge_send,
    edge_recv,
    lev_send,
    lev_recv,
    row_send,
    row_recv,
    rim_send,
    rim_recv,
):
    shots, slabs, cells, size_y, size_z, count = dims
    me_shot = lax.axis_index("shot")
    me_gx = lax.axis_index("gx")
    has_left = me_gx > 0
    has_right = me_gx < slabs - 1
    left = {"gx": me_gx - 1}
    right = {"gx": me_gx + 1}
    coarse_x, coarse_y, coarse_z = cells // 4, size_y // 4, size_z // 4
    own_rows = coarse_y // shots
    window = own_rows + 2
    H = HMAX
    lev = (first_lev, second_lev)

    loads = [
        pltpu.make_async_copy(sn_ref.at[0], now.at[0, pl.ds(1, cells)], load_sem.at[0]),
        pltpu.make_async_copy(rn_ref.at[0], now.at[1, pl.ds(1, cells)], load_sem.at[1]),
        pltpu.make_async_copy(sp_ref.at[0], prev.at[0], load_sem.at[2]),
        pltpu.make_async_copy(rp_ref.at[0], prev.at[1], load_sem.at[3]),
        pltpu.make_async_copy(courant_ref, cour, load_sem.at[4]),
    ]
    for load in loads:
        load.start()

    barrier = pltpu.get_barrier_semaphore()
    for step in range(1, shots):
        pl.semaphore_signal(
            barrier,
            inc=1,
            device_id={"shot": lax.rem(me_shot + step, shots)},
            device_id_type=MESH,
        )

    @pl.when(has_left)
    def _():
        pl.semaphore_signal(barrier, inc=1, device_id=left, device_id_type=MESH)

    @pl.when(has_right)
    def _():
        pl.semaphore_signal(barrier, inc=1, device_id=right, device_id_type=MESH)

    pl.semaphore_wait(
        barrier, shots - 1 + has_left.astype(jnp.int32) + has_right.astype(jnp.int32)
    )

    def remote(src, dst, send, recv, target):
        return pltpu.make_async_remote_copy(
            src_ref=src,
            dst_ref=dst,
            send_sem=send,
            recv_sem=recv,
            device_id=target,
            device_id_type=MESH,
        )

    def edge_copy(field, side):
        source = (sn_ref, rn_ref)[field]
        plane, place = ((0, cells + 1), (cells - 1, 0))[side]
        return remote(
            source.at[0, pl.ds(plane, 1)],
            now.at[field, pl.ds(place, 1)],
            edge_send.at[field, side],
            edge_recv.at[field, side],
            (left, right)[side],
        )

    def level_copy(step, field, side, part):
        if side == 0:
            first, size = ((1, H - 1), (0, 1))[part]
            place = H + cells + first
        else:
            first, size = ((cells - H, H - 1), (cells - 1, 1))[part]
            place = first - cells + H
        return remote(
            lev[step].at[field, pl.ds(H + first, size)],
            lev[step].at[field, pl.ds(place, size)],
            lev_send.at[step, field, side, part],
            lev_recv.at[step, field, side, part],
            (left, right)[side],
        )

    def goes(side):
        return (has_left, has_right)[side]

    def comes(side):
        return (has_right, has_left)[side]

    def start(copy, side):
        @pl.when(goes(side))
        def _():
            copy.start()

    def wait_send(copy, side):
        @pl.when(goes(side))
        def _():
            copy.wait_send()

    def wait_recv(copy, side):
        @pl.when(comes(side))
        def _():
            copy.wait_recv()

    for field in range(2):
        for side in range(2):
            start(edge_copy(field, side), side)

    zero_plane = jnp.zeros((size_y, size_z), jnp.float32)

    @pl.when(jnp.logical_not(has_left))
    def _():
        for field in range(2):
            now[field, 0] = zero_plane
            for step in range(2):
                lev[step][field, 0:H] = jnp.zeros((H, size_y, size_z), jnp.float32)

    @pl.when(jnp.logical_not(has_right))
    def _():
        for field in range(2):
            now[field, cells + 1] = zero_plane
            for step in range(2):
                lev[step][field, H + cells : H + cells + H] = jnp.zeros(
                    (H, size_y, size_z), jnp.float32
                )

    z_bits = size_z.bit_length() - 1
    first_row = me_gx * (cells * size_y)

    def columns(cell, amps):
        lanes = cell.shape[-1]
        z_of = jnp.bitwise_and(cell, size_z - 1)
        hit = lax.broadcasted_iota(jnp.int32, (size_z, lanes), 0) == z_of
        pieces = []
        for amp in amps:
            high = amp.astype(jnp.bfloat16).astype(jnp.float32)
            for piece in (high, amp - high):
                pieces.append(jnp.where(hit, piece, 0.0).astype(jnp.bfloat16))
        return jnp.concatenate(pieces, axis=0)

    def spread(field, cell, amps):
        lanes = cell.shape[-1]
        right_side = columns(cell, amps)
        row_of = jnp.right_shift(cell, z_bits) - first_row
        block = 4 * size_y

        def body(step, carry):
            first = step * block
            row = lax.broadcasted_iota(jnp.int32, (block, lanes), 0) + first
            hit = jnp.where(row == row_of, 1.0, 0.0).astype(jnp.bfloat16)
            value = lax.dot_general(
                hit, right_side, (((1,), (1,)), ((), ())), preferred_element_type=jnp.float32
            )
            at = pl.ds(pl.multiple_of(first, block), block)
            inj[0, field, at] = value[:, 0:size_z] + value[:, size_z : 2 * size_z]
            inj[1, field, at] = value[:, 2 * size_z : 3 * size_z] + value[:, 3 * size_z :]
            return carry

        lax.fori_loop(0, cells * size_y // block, body, 0)

    few = scells_ref.shape[-1]
    padi[...] = jnp.full(padi.shape, -1, jnp.int32)
    pads[...] = jnp.zeros(pads.shape, jnp.float32)
    padi[0:1, 0:few] = scells_ref[...]
    pads[0:2, 0:few] = wavelet_ref[0]
    spread(0, padi[0:1], (pads[0:1], pads[1:2]))
    spread(1, rcells_ref[...], (rdata_ref[0, 0:1], rdata_ref[0, 1:2]))

    row_index = lax.broadcasted_iota(jnp.int32, (size_y, size_z), 0)
    lane_index = lax.broadcasted_iota(jnp.int32, (size_y, size_z), 1)

    def advance(before, low, center, high, speed, source):
        total = low + high
        total = total + jnp.where(row_index == 0, 0.0, pltpu.roll(center, 1, 0))
        total = total + jnp.where(row_index == size_y - 1, 0.0, pltpu.roll(center, size_y - 1, 0))
        total = total + jnp.where(lane_index == 0, 0.0, pltpu.roll(center, 1, 1))
        total = total + jnp.where(lane_index == size_z - 1, 0.0, pltpu.roll(center, size_z - 1, 1))
        return 2.0 * center - before + speed * (total - 6.0 * center) + source

    def first_level(x):
        speed = cour[x]
        for field in range(2):
            source = inj[0, field, pl.ds(pl.multiple_of(x * size_y, size_y), size_y)]
            lev[0][field, H + x] = advance(
                prev[field, x], now[field, x], now[field, x + 1], now[field, x + 2], speed, source
            )

    def second_level(x):
        speed = cour[x]
        for field in range(2):
            source = inj[1, field, pl.ds(pl.multiple_of(x * size_y, size_y), size_y)]
            lev[1][field, H + x] = advance(
                now[field, x + 1],
                lev[0][field, H + x - 1],
                lev[0][field, H + x],
                lev[0][field, H + x + 1],
                speed,
                source,
            )

    def planes(one, first, last):
        def body(x, carry):
            one(x)
            return carry

        lax.fori_loop(first, last, body, 0)

    def inner_planes(step, one):
        planes(one, cells - H, cells - 1)
        for field in range(2):
            start(level_copy(step, field, 1, 0), 1)
        planes(one, 1, cells - H)
        for field in range(2):
            start(level_copy(step, field, 0, 0), 0)

    def outer_planes(step, one):
        one(0)
        one(cells - 1)
        for field in range(2):
            for side in range(2):
                start(level_copy(step, field, side, 1), side)

    for load in loads:
        load.wait()
    inner_planes(0, first_level)
    for field in range(2):
        for side in range(2):
            wait_recv(edge_copy(field, side), side)
    outer_planes(0, first_level)
    inner_planes(1, second_level)
    for field in range(2):
        for side in range(2):
            wait_recv(level_copy(0, field, side, 1), side)
    outer_planes(1, second_level)

    def products(step):
        def body(item, carry):
            which = item // coarse_x
            block = item % coarse_x
            offset = offsets_ref[which]
            total = (
                lev[step][0, H + offset + block * 4] * lev[step][1, H - offset + block * 4]
            )
            for inner in range(1, 4):
                total = total + (
                    lev[step][0, H + offset + block * 4 + inner]
                    * lev[step][1, H - offset + block * 4 + inner]
                )
            if step == 0:
                acc[which, block] = total
            else:
                acc[which, block] = acc[which, block] + total
            return carry

        lax.fori_loop(0, count * coarse_x, body, 0)

    for field in range(2):
        for side in range(2):
            wait_recv(level_copy(0, field, side, 0), side)
    products(0)
    for field in range(2):
        for side in range(2):
            wait_recv(level_copy(1, field, side, 0), side)
            wait_recv(level_copy(1, field, side, 1), side)
    products(1)

    lanes = coarse_x * coarse_z
    deep = coarse_x * size_z
    z_row = lax.broadcasted_iota(jnp.int32, (deep, lanes), 0)
    z_col = lax.broadcasted_iota(jnp.int32, (deep, lanes), 1)
    mean = jnp.where(jnp.right_shift(z_row, 2) == z_col, 1.0 / 64.0, 0.0)
    wide = []
    for which in range(count):
        by_x = []
        for block in range(coarse_x):
            total = acc[which, block, pl.ds(0, coarse_y, stride=4)]
            for inner in range(1, 4):
                total = total + acc[which, block, pl.ds(inner, coarse_y, stride=4)]
            by_x.append(total)
        wide.append(jnp.concatenate(by_x, axis=1))
    coarse = jnp.dot(
        jnp.concatenate(wide, axis=0),
        mean,
        precision=lax.Precision.HIGHEST,
        preferred_element_type=jnp.float32,
    )
    rows[0] = jnp.zeros((count, lanes), jnp.float32)
    rows[coarse_y + 1] = jnp.zeros((count, lanes), jnp.float32)
    for which in range(count):
        for y in range(coarse_y):
            line = which * coarse_y + y
            rows[1 + y, which : which + 1] = coarse[line : line + 1]

    def row_copy(step):
        target = lax.rem(me_shot + step, shots)
        return remote(
            rows.at[pl.ds(target * own_rows, window)],
            parts.at[step],
            row_send.at[step],
            row_recv.at[step],
            {"shot": target},
        )

    for step in range(1, shots):
        row_copy(step).start()
    total = rows[pl.ds(me_shot * own_rows, window)]
    for step in range(1, shots):
        row_copy(step).wait_recv()
        total = total + parts[step]
    summed[1] = jnp.zeros(summed.shape[1:], jnp.float32)
    summed[1, :, 0:count] = total

    def rim_copy(side):
        return remote(
            summed.at[1],
            summed.at[(2, 0)[side]],
            rim_send.at[side],
            rim_recv.at[side],
            (left, right)[side],
        )

    for side in range(2):
        start(rim_copy(side), side)

    @pl.when(jnp.logical_not(has_left))
    def _():
        summed[0] = jnp.zeros(summed.shape[1:], jnp.float32)

    @pl.when(jnp.logical_not(has_right))
    def _():
        summed[2] = jnp.zeros(summed.shape[1:], jnp.float32)

    for side in range(2):
        wait_recv(rim_copy(side), side)

    flat = (window * 16, lanes)
    lane = lax.broadcasted_iota(jnp.int32, flat, 1)
    z_lane = jnp.bitwise_and(lane, coarse_z - 1)
    low, own, high = (summed[place].reshape(flat) for place in range(3))
    shifted = (
        jnp.where(lane < coarse_z, pltpu.roll(low, coarse_z, 1), pltpu.roll(own, coarse_z, 1)),
        own,
        jnp.where(
            lane >= lanes - coarse_z,
            pltpu.roll(high, lanes - coarse_z, 1),
            pltpu.roll(own, lanes - coarse_z, 1),
        ),
    )
    for a in range(3):
        patches[a * 3] = jnp.where(z_lane == 0, 0.0, pltpu.roll(shifted[a], 1, 1))
        patches[a * 3 + 1] = shifted[a]
        patches[a * 3 + 2] = jnp.where(
            z_lane == coarse_z - 1, 0.0, pltpu.roll(shifted[a], lanes - 1, 1)
        )
    for y in range(own_rows):
        tall = jnp.concatenate([patches[k, y * 16 : y * 16 + 48] for k in range(9)], axis=0)
        out_ref[:, y * lanes : (y + 1) * lanes] = jnp.dot(
            weight_ref[...],
            tall,
            precision=lax.Precision.HIGHEST,
            preferred_element_type=jnp.float32,
        )

    for field in range(2):
        for side in range(2):
            wait_send(edge_copy(field, side), side)
            for step in range(2):
                for part in range(2):
                    wait_send(level_copy(step, field, side, part), side)
    for step in range(1, shots):
        row_copy(step).wait_send()
    for side in range(2):
        wait_send(rim_copy(side), side)


def local(
    source_prev,
    source_now,
    receiver_prev,
    receiver_now,
    courant,
    source_cells,
    wavelet,
    receiver_cells,
    receiver_data,
    offsets,
    conv_weight,
    conv_bias,
):
    cells, size_y, size_z = courant.shape
    shots, slabs = lax.axis_size("shot"), lax.axis_size("gx")
    count = offsets.shape[0]
    channels = conv_weight.shape[0]
    coarse_x, coarse_y, coarse_z = cells // 4, size_y // 4, size_z // 4
    own_rows = coarse_y // shots
    window = own_rows + 2
    lanes = coarse_x * coarse_z
    weight = jnp.pad(
        conv_weight.transpose(0, 2, 4, 3, 1), ((0, 0), (0, 0), (0, 0), (0, 0), (0, 16 - count))
    ).reshape(channels, 27 * 16)

    anywhere = pl.BlockSpec(memory_space=pl.ANY)
    vmem = pl.BlockSpec(memory_space=pltpu.VMEM)
    smem = pl.BlockSpec(memory_space=pltpu.SMEM)
    f32 = jnp.float32
    result = pl.pallas_call(
        functools.partial(kernel, (shots, slabs, cells, size_y, size_z, count)),
        out_shape=jax.ShapeDtypeStruct((channels, own_rows * lanes), f32),
        in_specs=[anywhere] * 5 + [vmem] * 4 + [smem, vmem],
        out_specs=vmem,
        scratch_shapes=[
            pltpu.VMEM((2, cells + 2, size_y, size_z), f32),
            pltpu.VMEM((2, cells, size_y, size_z), f32),
            pltpu.VMEM((cells, size_y, size_z), f32),
            pltpu.VMEM((2, cells + 2 * HMAX, size_y, size_z), f32),
            pltpu.VMEM((2, cells + 2 * HMAX, size_y, size_z), f32),
            pltpu.VMEM((2, 2, cells * size_y, size_z), f32),
            pltpu.VMEM((count, coarse_x, size_y, size_z), f32),
            pltpu.VMEM((8, 128), f32),
            pltpu.VMEM((8, 128), jnp.int32),
            pltpu.VMEM((coarse_y + 2, count, lanes), f32),
            pltpu.VMEM((shots, window, count, lanes), f32),
            pltpu.VMEM((3, window, 16, lanes), f32),
            pltpu.VMEM((9, window * 16, lanes), f32),
            pltpu.SemaphoreType.DMA((5,)),
            pltpu.SemaphoreType.DMA((2, 2)),
            pltpu.SemaphoreType.DMA((2, 2)),
            pltpu.SemaphoreType.DMA((2, 2, 2, 2)),
            pltpu.SemaphoreType.DMA((2, 2, 2, 2)),
            pltpu.SemaphoreType.DMA((shots,)),
            pltpu.SemaphoreType.DMA((shots,)),
            pltpu.SemaphoreType.DMA((2,)),
            pltpu.SemaphoreType.DMA((2,)),
        ],
        compiler_params=pltpu.CompilerParams(
            collective_id=0, has_side_effects=True, vmem_limit_bytes=32 * 1024 * 1024
        ),
        cost_estimate=pl.CostEstimate(
            flops=1_500_000_000, bytes_accessed=3_000_000, transcendentals=0
        ),
    )(
        source_prev,
        source_now,
        receiver_prev,
        receiver_now,
        courant,
        source_cells,
        wavelet,
        receiver_cells,
        receiver_data,
        offsets,
        weight,
    )
    result = result.reshape(channels, own_rows, coarse_x, coarse_z).transpose(0, 2, 1, 3)
    return result.reshape(channels, coarse_x, own_rows * coarse_z) + conv_bias[:, None, None]


def solution(mesh):
    in_specs = (
        P("shot", "gx", None, None),
        P("shot", "gx", None, None),
        P("shot", "gx", None, None),
        P("shot", "gx", None, None),
        P("gx", None, None),
        P("shot", None),
        P("shot", None, None),
        P("shot", None),
        P("shot", None, None),
        P(),
        P(),
        P(),
    )
    out_specs = P(None, "gx", "shot")
    return jax.shard_map(local, mesh=mesh, in_specs=in_specs, out_specs=out_specs, check_vma=False)
```

```python
import functools

import jax
import jax.numpy as jnp
from jax import lax
from jax.experimental import pallas as pl
from jax.experimental.pallas import tpu as pltpu
from jax.sharding import PartitionSpec as P

HMAX = 8
HALVES = 2
MESH = pl.DeviceIdType.MESH


def kernel(
    dims,
    sp_ref,
    sn_ref,
    rp_ref,
    rn_ref,
    courant_ref,
    scells_ref,
    wavelet_ref,
    rcells_ref,
    rdata_ref,
    offsets_ref,
    weight_ref,
    bias_ref,
    out_ref,
    now,
    prev,
    cour,
    first_lev,
    second_low,
    second_high,
    inj,
    acc,
    pads,
    padi,
    rows,
    parts,
    summed,
    patches,
    conv_in,
    tall,
    load_sem,
    edge_send,
    edge_recv,
    lev_send,
    lev_recv,
    row_send,
    row_recv,
    rim_send,
    rim_recv,
    late_send,
    late_recv,
):
    shots, slabs, cells, size_y, size_z, count = dims
    me_shot = lax.axis_index("shot")
    me_gx = lax.axis_index("gx")
    has_left = me_gx > 0
    has_right = me_gx < slabs - 1
    left = {"gx": me_gx - 1}
    right = {"gx": me_gx + 1}
    coarse_x, coarse_y, coarse_z = cells // 4, size_y // 4, size_z // 4
    own_rows = coarse_y // shots
    window = own_rows + 2
    H = HMAX
    second = (second_low, second_high)
    half_y = size_y // HALVES
    half_rows = coarse_y // HALVES

    loads = [
        pltpu.make_async_copy(sn_ref.at[0], now.at[0, pl.ds(1, cells)], load_sem.at[0]),
        pltpu.make_async_copy(rn_ref.at[0], now.at[1, pl.ds(1, cells)], load_sem.at[1]),
        pltpu.make_async_copy(sp_ref.at[0], prev.at[0], load_sem.at[2]),
        pltpu.make_async_copy(rp_ref.at[0], prev.at[1], load_sem.at[3]),
        pltpu.make_async_copy(courant_ref, cour, load_sem.at[4]),
    ]
    for load in loads:
        load.start()
    weight_load = pltpu.make_async_copy(weight_ref, conv_in, load_sem.at[5])
    weight_load.start()

    barrier = pltpu.get_barrier_semaphore()
    for step in range(1, shots):
        pl.semaphore_signal(
            barrier,
            inc=1,
            device_id={"shot": lax.rem(me_shot + step, shots)},
            device_id_type=MESH,
        )

    @pl.when(has_left)
    def _():
        pl.semaphore_signal(barrier, inc=1, device_id=left, device_id_type=MESH)

    @pl.when(has_right)
    def _():
        pl.semaphore_signal(barrier, inc=1, device_id=right, device_id_type=MESH)

    def remote(src, dst, send, recv, target):
        return pltpu.make_async_remote_copy(
            src_ref=src,
            dst_ref=dst,
            send_sem=send,
            recv_sem=recv,
            device_id=target,
            device_id_type=MESH,
        )

    def edge_copy(field, side):
        source = (sn_ref, rn_ref)[field]
        plane, place = ((0, cells + 1), (cells - 1, 0))[side]
        return remote(
            source.at[0, pl.ds(plane, 1)],
            now.at[field, pl.ds(place, 1)],
            edge_send.at[field, side],
            edge_recv.at[field, side],
            (left, right)[side],
        )

    def place_of(side, part):
        if side == 0:
            first, size = ((1, H - 1), (0, 1))[part]
            return first, size, H + cells + first
        first, size = ((cells - H, H - 1), (cells - 1, 1))[part]
        return first, size, first - cells + H

    def first_copy(field, side, part):
        first, size, place = place_of(side, part)
        return remote(
            first_lev.at[field, pl.ds(H + first, size)],
            first_lev.at[field, pl.ds(place, size)],
            lev_send.at[field, side, part],
            lev_recv.at[field, side, part],
            (left, right)[side],
        )

    def second_copy(half, field, side, part):
        first, size, place = place_of(side, part)
        return remote(
            second[half].at[field, pl.ds(H + first, size)],
            second[half].at[field, pl.ds(place, size)],
            late_send.at[half, field, side, part],
            late_recv.at[half, field, side, part],
            (left, right)[side],
        )

    both = [(field, side) for field in range(2) for side in range(2)]

    def goes(side):
        return (has_left, has_right)[side]

    def comes(side):
        return (has_right, has_left)[side]

    def start(copy, side):
        @pl.when(goes(side))
        def _():
            copy.start()

    def wait_send(copy, side):
        @pl.when(goes(side))
        def _():
            copy.wait_send()

    def wait_recv(copy, side):
        @pl.when(comes(side))
        def _():
            copy.wait_recv()

    zero_plane = jnp.zeros((size_y, size_z), jnp.float32)

    def clear(plane, place):
        for field in range(2):
            now[field, plane] = zero_plane
            first_lev[field, place : place + H] = jnp.zeros((H, size_y, size_z), jnp.float32)
            for half in range(HALVES):
                second[half][field, place : place + H] = jnp.zeros(
                    (H, half_y, size_z), jnp.float32
                )

    @pl.when(jnp.logical_not(has_left))
    def _():
        clear(0, 0)

    @pl.when(jnp.logical_not(has_right))
    def _():
        clear(cells + 1, H + cells)

    z_bits = size_z.bit_length() - 1
    first_row = me_gx * (cells * size_y)

    def spread(step, field, cell, amp):
        lanes = cell.shape[-1]
        z_of = jnp.bitwise_and(cell, size_z - 1)
        there = lax.broadcasted_iota(jnp.int32, (size_z, lanes), 0) == z_of
        high = amp.astype(jnp.bfloat16).astype(jnp.float32)
        pieces = [
            jnp.where(there, piece, 0.0).astype(jnp.bfloat16) for piece in (high, amp - high)
        ]
        right_side = jnp.concatenate(pieces, axis=0)
        row_of = jnp.right_shift(cell, z_bits) - first_row
        block = 4 * size_y

        def body(item, carry):
            first = item * block
            row = lax.broadcasted_iota(jnp.int32, (block, lanes), 0) + first
            hit = jnp.where(row == row_of, 1.0, 0.0).astype(jnp.bfloat16)
            value = lax.dot_general(
                hit, right_side, (((1,), (1,)), ((), ())), preferred_element_type=jnp.float32
            )
            at = pl.ds(pl.multiple_of(first, block), block)
            inj[step, field, at] = value[:, 0:size_z] + value[:, size_z:]
            return carry

        lax.fori_loop(0, cells * size_y // block, body, 0)

    few = scells_ref.shape[-1]
    padi[...] = jnp.full(padi.shape, -1, jnp.int32)
    pads[...] = jnp.zeros(pads.shape, jnp.float32)
    padi[0:1, 0:few] = scells_ref[...]
    pads[0:2, 0:few] = wavelet_ref[0]

    def injection(step):
        spread(step, 0, padi[0:1], pads[step : step + 1])
        spread(step, 1, rcells_ref[...], rdata_ref[0, step : step + 1])

    injection(0)

    pl.semaphore_wait(
        barrier, shots - 1 + has_left.astype(jnp.int32) + has_right.astype(jnp.int32)
    )

    for field, side in both:
        start(edge_copy(field, side), side)

    row_index = lax.broadcasted_iota(jnp.int32, (size_y, size_z), 0)
    lane_index = lax.broadcasted_iota(jnp.int32, (size_y, size_z), 1)

    def advance(before, low, center, high, speed, source):
        total = low + high
        total = total + jnp.where(row_index == 0, 0.0, pltpu.roll(center, 1, 0))
        total = total + jnp.where(row_index == size_y - 1, 0.0, pltpu.roll(center, size_y - 1, 0))
        total = total + jnp.where(lane_index == 0, 0.0, pltpu.roll(center, 1, 1))
        total = total + jnp.where(lane_index == size_z - 1, 0.0, pltpu.roll(center, size_z - 1, 1))
        return 2.0 * center - before + speed * (total - 6.0 * center) + source

    def first_level(x):
        speed = cour[x]
        for field in range(2):
            source = inj[0, field, pl.ds(pl.multiple_of(x * size_y, size_y), size_y)]
            first_lev[field, H + x] = advance(
                prev[field, x], now[field, x], now[field, x + 1], now[field, x + 2], speed, source
            )

    def second_level(x):
        speed = cour[x]
        for field in range(2):
            source = inj[1, field, pl.ds(pl.multiple_of(x * size_y, size_y), size_y)]
            value = advance(
                now[field, x + 1],
                first_lev[field, H + x - 1],
                first_lev[field, H + x],
                first_lev[field, H + x + 1],
                speed,
                source,
            )
            for half in range(HALVES):
                second[half][field, H + x] = value[half * half_y : (half + 1) * half_y]

    def planes(one, first, last):
        def body(x, carry):
            one(x)
            return carry

        lax.fori_loop(first, last, body, 0, unroll=True)

    for load in loads:
        load.wait()
    planes(first_level, cells - H, cells - 1)
    for field in range(2):
        start(first_copy(field, 1, 0), 1)
    planes(first_level, 1, cells - H)
    for field in range(2):
        start(first_copy(field, 0, 0), 0)
    for field, side in both:
        wait_recv(edge_copy(field, side), side)
    first_level(0)
    first_level(cells - 1)
    for field, side in both:
        start(first_copy(field, side, 1), side)

    injection(1)
    planes(second_level, cells - H, cells - 1)
    for field in range(2):
        start(second_copy(0, field, 1, 0), 1)
    planes(second_level, 1, cells - H)
    for field in range(2):
        start(second_copy(0, field, 0, 0), 0)
    for field, side in both:
        wait_recv(first_copy(field, side, 1), side)
    second_level(0)
    second_level(cells - 1)
    for half in range(HALVES):
        for field, side in both:
            start(second_copy(half, field, side, 1), side)
    for field, side in both:
        start(second_copy(1, field, side, 0), side)

    weight_load.wait()
    tall[...] = jnp.zeros(tall.shape, jnp.float32)
    for which in range(count):
        for a in range(3):
            for b in range(3):
                for c in range(3):
                    line = ((a * 3 + c) * 3 + b) * 16 + which
                    tall[line : line + 1] = conv_in[which, a, b, c : c + 1]
    line = 13 * 16 + count
    tall[line : line + 1] = bias_ref[...]
    matrix = tall[...].T

    def products(level, rows_here, first):
        def body(which, carry):
            offset = offsets_ref[which]
            for block in range(coarse_x):
                total = None
                for inner in range(4):
                    x = H + block * 4 + inner
                    term = level[0, x + offset] * level[1, x - offset]
                    total = term if total is None else total + term
                if first:
                    acc[which, block] = total
                else:
                    acc[which, block, rows_here] = acc[which, block, rows_here] + total
            return carry

        lax.fori_loop(0, count, body, 0)

    lanes = coarse_x * coarse_z
    deep = coarse_x * size_z
    z_row = lax.broadcasted_iota(jnp.int32, (deep, lanes), 0)
    z_col = lax.broadcasted_iota(jnp.int32, (deep, lanes), 1)
    mean = jnp.where(jnp.right_shift(z_row, 2) == z_col, 1.0 / 64.0, 0.0)
    rows[0] = jnp.zeros((count, lanes), jnp.float32)
    rows[coarse_y + 1] = jnp.zeros((count, lanes), jnp.float32)

    def means(half):
        wide = []
        for which in range(count):
            by_x = []
            for block in range(coarse_x):
                total = None
                for inner in range(4):
                    term = acc[which, block, pl.ds(half * half_y + inner, half_rows, stride=4)]
                    total = term if total is None else total + term
                by_x.append(total)
            wide.append(jnp.concatenate(by_x, axis=1))
        coarse = jnp.dot(
            jnp.concatenate(wide, axis=0),
            mean,
            precision=lax.Precision.HIGHEST,
            preferred_element_type=jnp.float32,
        )
        for which in range(count):
            for y in range(half_rows):
                line = which * half_rows + y
                rows[1 + half * half_rows + y, which : which + 1] = coarse[line : line + 1]

    def row_copy(source, target):
        return remote(
            rows.at[pl.ds(target * own_rows, window)],
            parts.at[source],
            row_send.at[target],
            row_recv.at[source],
            {"shot": target},
        )

    def send_rows(targets):
        for target in targets:

            @pl.when(me_shot != target)
            def _():
                row_copy(me_shot, target).start()

    for field, side in both:
        wait_recv(first_copy(field, side, 0), side)
    products(first_lev, slice(0, size_y), True)
    sent = 0
    for half in range(HALVES):
        for field, side in both:
            wait_recv(second_copy(half, field, side, 1), side)
            wait_recv(second_copy(half, field, side, 0), side)
        products(second[half], slice(half * half_y, (half + 1) * half_y), False)
        means(half)
        done = shots if half == HALVES - 1 else ((half + 1) * half_rows + 1 - window) // own_rows + 1
        send_rows(range(sent, done))
        sent = done
    parts[me_shot] = rows[pl.ds(me_shot * own_rows, window)]
    total = None
    for source in range(shots):

        @pl.when(me_shot != source)
        def _():
            row_copy(source, source).wait_recv()

        total = parts[source] if total is None else total + parts[source]
    summed[1] = jnp.zeros(summed.shape[1:], jnp.float32)
    summed[1, :, 0:count] = total
    summed[1, :, count : count + 1] = jnp.ones((window, 1, lanes), jnp.float32)

    def rim_copy(side):
        return remote(
            summed.at[1],
            summed.at[(2, 0)[side]],
            rim_send.at[side],
            rim_recv.at[side],
            (left, right)[side],
        )

    for side in range(2):
        start(rim_copy(side), side)

    @pl.when(jnp.logical_not(has_left))
    def _():
        summed[0] = jnp.zeros(summed.shape[1:], jnp.float32)

    @pl.when(jnp.logical_not(has_right))
    def _():
        summed[2] = jnp.zeros(summed.shape[1:], jnp.float32)

    for side in range(2):
        wait_recv(rim_copy(side), side)

    flat = (window * 16, lanes)
    lane = lax.broadcasted_iota(jnp.int32, flat, 1)
    z_lane = jnp.bitwise_and(lane, coarse_z - 1)
    low, own, high = (summed[place].reshape(flat) for place in range(3))
    shifted = (
        jnp.where(lane < coarse_z, pltpu.roll(low, coarse_z, 1), pltpu.roll(own, coarse_z, 1)),
        own,
        jnp.where(
            lane >= lanes - coarse_z,
            pltpu.roll(high, lanes - coarse_z, 1),
            pltpu.roll(own, lanes - coarse_z, 1),
        ),
    )
    for a in range(3):
        patches[a * 3] = jnp.where(z_lane == 0, 0.0, pltpu.roll(shifted[a], 1, 1))
        patches[a * 3 + 1] = shifted[a]
        patches[a * 3 + 2] = jnp.where(
            z_lane == coarse_z - 1, 0.0, pltpu.roll(shifted[a], lanes - 1, 1)
        )
    for y in range(own_rows):
        deep_rows = jnp.concatenate([patches[k, y * 16 : y * 16 + 48] for k in range(9)], axis=0)
        out_ref[:, y * lanes : (y + 1) * lanes] = jnp.dot(
            matrix,
            deep_rows,
            precision=lax.Precision.HIGHEST,
            preferred_element_type=jnp.float32,
        )

    for field, side in both:
        wait_send(edge_copy(field, side), side)
        for part in range(2):
            wait_send(first_copy(field, side, part), side)
            for half in range(HALVES):
                wait_send(second_copy(half, field, side, part), side)
    for target in range(shots):

        @pl.when(me_shot != target)
        def _():
            row_copy(me_shot, target).wait_send()

    for side in range(2):
        wait_send(rim_copy(side), side)


def local(
    source_prev,
    source_now,
    receiver_prev,
    receiver_now,
    courant,
    source_cells,
    wavelet,
    receiver_cells,
    receiver_data,
    offsets,
    conv_weight,
    conv_bias,
):
    cells, size_y, size_z = courant.shape
    shots, slabs = lax.axis_size("shot"), lax.axis_size("gx")
    count = offsets.shape[0]
    channels = conv_weight.shape[0]
    coarse_x, coarse_y, coarse_z = cells // 4, size_y // 4, size_z // 4
    own_rows = coarse_y // shots
    window = own_rows + 2
    lanes = coarse_x * coarse_z
    anywhere = pl.BlockSpec(memory_space=pltpu.HBM)
    vmem = pl.BlockSpec(memory_space=pltpu.VMEM)
    smem = pl.BlockSpec(memory_space=pltpu.SMEM)
    f32 = jnp.float32
    result = pl.pallas_call(
        functools.partial(kernel, (shots, slabs, cells, size_y, size_z, count)),
        out_shape=jax.ShapeDtypeStruct((channels, own_rows * lanes), f32),
        in_specs=[anywhere] * 5 + [vmem] * 4 + [smem, anywhere, vmem],
        out_specs=vmem,
        scratch_shapes=[
            pltpu.VMEM((2, cells + 2, size_y, size_z), f32),
            pltpu.VMEM((2, cells, size_y, size_z), f32),
            pltpu.VMEM((cells, size_y, size_z), f32),
            pltpu.VMEM((2, cells + 2 * HMAX, size_y, size_z), f32),
            pltpu.VMEM((2, cells + 2 * HMAX, size_y // HALVES, size_z), f32),
            pltpu.VMEM((2, cells + 2 * HMAX, size_y // HALVES, size_z), f32),
            pltpu.VMEM((2, 2, cells * size_y, size_z), f32),
            pltpu.VMEM((count, coarse_x, size_y, size_z), f32),
            pltpu.VMEM((8, 128), f32),
            pltpu.VMEM((8, 128), jnp.int32),
            pltpu.VMEM((coarse_y + 2, count, lanes), f32),
            pltpu.VMEM((shots, window, count, lanes), f32),
            pltpu.VMEM((3, window, 16, lanes), f32),
            pltpu.VMEM((9, window * 16, lanes), f32),
            pltpu.VMEM((count, 3, 3, 3, channels), f32),
            pltpu.VMEM((27 * 16, channels), f32),
            pltpu.SemaphoreType.DMA((6,)),
            pltpu.SemaphoreType.DMA((2, 2)),
            pltpu.SemaphoreType.DMA((2, 2)),
            pltpu.SemaphoreType.DMA((2, 2, 2)),
            pltpu.SemaphoreType.DMA((2, 2, 2)),
            pltpu.SemaphoreType.DMA((shots,)),
            pltpu.SemaphoreType.DMA((shots,)),
            pltpu.SemaphoreType.DMA((2,)),
            pltpu.SemaphoreType.DMA((2,)),
            pltpu.SemaphoreType.DMA((HALVES, 2, 2, 2)),
            pltpu.SemaphoreType.DMA((HALVES, 2, 2, 2)),
        ],
        compiler_params=pltpu.CompilerParams(
            collective_id=0, has_side_effects=True, vmem_limit_bytes=64 * 1024 * 1024 - 256 * 1024
        ),
        cost_estimate=pl.CostEstimate(
            flops=1_500_000_000, bytes_accessed=3_000_000, transcendentals=0
        ),
    )(
        source_prev,
        source_now,
        receiver_prev,
        receiver_now,
        courant,
        source_cells,
        wavelet,
        receiver_cells,
        receiver_data,
        offsets,
        conv_weight.transpose(1, 2, 3, 4, 0),
        conv_bias.reshape(1, channels),
    )
    result = result.reshape(channels, own_rows, coarse_x, coarse_z).transpose(0, 2, 1, 3)
    return result.reshape(channels, coarse_x, own_rows * coarse_z)


def solution(mesh):
    in_specs = (
        P("shot", "gx", None, None),
        P("shot", "gx", None, None),
        P("shot", "gx", None, None),
        P("shot", "gx", None, None),
        P("gx", None, None),
        P("shot", None),
        P("shot", None, None),
        P("shot", None),
        P("shot", None, None),
        P(),
        P(),
        P(),
    )
    out_specs = P(None, "gx", "shot")
    return jax.shard_map(local, mesh=mesh, in_specs=in_specs, out_specs=out_specs, check_vma=False)
```

```python
import functools

import jax
import jax.numpy as jnp
from jax import lax
from jax.experimental import pallas as pl
from jax.experimental.pallas import tpu as pltpu
from jax.sharding import PartitionSpec as P

HMAX = 8
HALVES = 2
MESH = pl.DeviceIdType.MESH


def kernel(
    dims,
    sp_ref,
    sn_ref,
    rp_ref,
    rn_ref,
    courant_ref,
    scells_ref,
    wavelet_ref,
    rcells_ref,
    rdata_ref,
    offsets_ref,
    weight_ref,
    bias_ref,
    out_ref,
    now,
    prev,
    cour,
    first_lev,
    second_low,
    second_high,
    inj,
    acc,
    pads,
    padi,
    rows,
    parts,
    summed,
    patches,
    conv_in,
    tall,
    load_sem,
    edge_send,
    edge_recv,
    lev_send,
    lev_recv,
    row_send,
    row_recv,
    rim_send,
    rim_recv,
    late_send,
    late_recv,
):
    shots, slabs, cells, size_y, size_z, count = dims
    me_shot = lax.axis_index("shot")
    me_gx = lax.axis_index("gx")
    has_left = me_gx > 0
    has_right = me_gx < slabs - 1
    left = {"gx": me_gx - 1}
    right = {"gx": me_gx + 1}
    coarse_x, coarse_y, coarse_z = cells // 4, size_y // 4, size_z // 4
    own_rows = coarse_y // shots
    window = own_rows + 2
    H = HMAX
    second = (second_low, second_high)
    half_y = size_y // HALVES
    half_rows = coarse_y // HALVES

    loads = [
        pltpu.make_async_copy(sn_ref.at[0], now.at[0, pl.ds(1, cells)], load_sem.at[0]),
        pltpu.make_async_copy(rn_ref.at[0], now.at[1, pl.ds(1, cells)], load_sem.at[1]),
        pltpu.make_async_copy(sp_ref.at[0], prev.at[0], load_sem.at[2]),
        pltpu.make_async_copy(rp_ref.at[0], prev.at[1], load_sem.at[3]),
        pltpu.make_async_copy(courant_ref, cour, load_sem.at[4]),
    ]
    for load in loads:
        load.start()
    weight_load = pltpu.make_async_copy(weight_ref, conv_in, load_sem.at[5])
    weight_load.start()

    barrier = pltpu.get_barrier_semaphore()
    for step in range(1, shots):
        pl.semaphore_signal(
            barrier,
            inc=1,
            device_id={"shot": lax.rem(me_shot + step, shots)},
            device_id_type=MESH,
        )

    @pl.when(has_left)
    def _():
        pl.semaphore_signal(barrier, inc=1, device_id=left, device_id_type=MESH)

    @pl.when(has_right)
    def _():
        pl.semaphore_signal(barrier, inc=1, device_id=right, device_id_type=MESH)

    def remote(src, dst, send, recv, target):
        return pltpu.make_async_remote_copy(
            src_ref=src,
            dst_ref=dst,
            send_sem=send,
            recv_sem=recv,
            device_id=target,
            device_id_type=MESH,
        )

    def edge_copy(field, side):
        source = (sn_ref, rn_ref)[field]
        plane, place = ((0, cells + 1), (cells - 1, 0))[side]
        return remote(
            source.at[0, pl.ds(plane, 1)],
            now.at[field, pl.ds(place, 1)],
            edge_send.at[field, side],
            edge_recv.at[field, side],
            (left, right)[side],
        )

    def place_of(side, part):
        if side == 0:
            first, size = ((1, H - 1), (0, 1))[part]
            return first, size, H + cells + first
        first, size = ((cells - H, H - 1), (cells - 1, 1))[part]
        return first, size, first - cells + H

    def first_copy(field, side, part):
        first, size, place = place_of(side, part)
        return remote(
            first_lev.at[field, pl.ds(H + first, size)],
            first_lev.at[field, pl.ds(place, size)],
            lev_send.at[field, side, part],
            lev_recv.at[field, side, part],
            (left, right)[side],
        )

    def second_copy(half, field, side, part):
        first, size, place = place_of(side, part)
        return remote(
            second[half].at[field, pl.ds(H + first, size)],
            second[half].at[field, pl.ds(place, size)],
            late_send.at[half, field, side, part],
            late_recv.at[half, field, side, part],
            (left, right)[side],
        )

    both = [(field, side) for field in range(2) for side in range(2)]

    def goes(side):
        return (has_left, has_right)[side]

    def comes(side):
        return (has_right, has_left)[side]

    def start(copy, side):
        @pl.when(goes(side))
        def _():
            copy.start()

    def wait_send(copy, side):
        @pl.when(goes(side))
        def _():
            copy.wait_send()

    def wait_recv(copy, side):
        @pl.when(comes(side))
        def _():
            copy.wait_recv()

    zero_plane = jnp.zeros((size_y, size_z), jnp.float32)

    def clear(plane, place):
        for field in range(2):
            now[field, plane] = zero_plane
            first_lev[field, place : place + H] = jnp.zeros((H, size_y, size_z), jnp.float32)
            for half in range(HALVES):
                second[half][field, place : place + H] = jnp.zeros(
                    (H, half_y, size_z), jnp.float32
                )

    @pl.when(jnp.logical_not(has_left))
    def _():
        clear(0, 0)

    @pl.when(jnp.logical_not(has_right))
    def _():
        clear(cells + 1, H + cells)

    z_bits = size_z.bit_length() - 1
    first_row = me_gx * (cells * size_y)

    def spread(step, field, cell, amp):
        lanes = cell.shape[-1]
        z_of = jnp.bitwise_and(cell, size_z - 1)
        there = lax.broadcasted_iota(jnp.int32, (size_z, lanes), 0) == z_of
        high = amp.astype(jnp.bfloat16).astype(jnp.float32)
        pieces = [
            jnp.where(there, piece, 0.0).astype(jnp.bfloat16) for piece in (high, amp - high)
        ]
        right_side = jnp.concatenate(pieces, axis=0)
        row_of = jnp.right_shift(cell, z_bits) - first_row
        block = 8 * size_y

        def body(item, carry):
            first = item * block
            row = lax.broadcasted_iota(jnp.int32, (block, lanes), 0) + first
            hit = jnp.where(row == row_of, 1.0, 0.0).astype(jnp.bfloat16)
            value = lax.dot_general(
                hit, right_side, (((1,), (1,)), ((), ())), preferred_element_type=jnp.float32
            )
            at = pl.ds(pl.multiple_of(first, block), block)
            inj[step, field, at] = value[:, 0:size_z] + value[:, size_z:]
            return carry

        lax.fori_loop(0, cells * size_y // block, body, 0, unroll=True)

    few = scells_ref.shape[-1]
    padi[...] = jnp.full(padi.shape, -1, jnp.int32)
    pads[...] = jnp.zeros(pads.shape, jnp.float32)
    padi[0:1, 0:few] = scells_ref[...]
    pads[0:2, 0:few] = wavelet_ref[0]

    def injection(step):
        spread(step, 0, padi[0:1], pads[step : step + 1])
        spread(step, 1, rcells_ref[...], rdata_ref[0, step : step + 1])

    injection(0)

    pl.semaphore_wait(
        barrier, shots - 1 + has_left.astype(jnp.int32) + has_right.astype(jnp.int32)
    )

    for field, side in both:
        start(edge_copy(field, side), side)

    row_index = lax.broadcasted_iota(jnp.int32, (size_y, size_z), 0)
    lane_index = lax.broadcasted_iota(jnp.int32, (size_y, size_z), 1)

    def advance(before, low, center, high, speed, source):
        total = low + high
        total = total + jnp.where(row_index == 0, 0.0, pltpu.roll(center, 1, 0))
        total = total + jnp.where(row_index == size_y - 1, 0.0, pltpu.roll(center, size_y - 1, 0))
        total = total + jnp.where(lane_index == 0, 0.0, pltpu.roll(center, 1, 1))
        total = total + jnp.where(lane_index == size_z - 1, 0.0, pltpu.roll(center, size_z - 1, 1))
        return 2.0 * center - before + speed * (total - 6.0 * center) + source

    def first_level(x):
        speed = cour[x]
        for field in range(2):
            source = inj[0, field, pl.ds(pl.multiple_of(x * size_y, size_y), size_y)]
            first_lev[field, H + x] = advance(
                prev[field, x], now[field, x], now[field, x + 1], now[field, x + 2], speed, source
            )

    def second_level(x):
        speed = cour[x]
        for field in range(2):
            source = inj[1, field, pl.ds(pl.multiple_of(x * size_y, size_y), size_y)]
            value = advance(
                now[field, x + 1],
                first_lev[field, H + x - 1],
                first_lev[field, H + x],
                first_lev[field, H + x + 1],
                speed,
                source,
            )
            for half in range(HALVES):
                second[half][field, H + x] = value[half * half_y : (half + 1) * half_y]

    def planes(one, first, last):
        def body(x, carry):
            one(x)
            return carry

        lax.fori_loop(first, last, body, 0, unroll=True)

    for load in loads:
        load.wait()
    planes(first_level, cells - H, cells - 1)
    for field in range(2):
        start(first_copy(field, 1, 0), 1)
    planes(first_level, 1, cells - H)
    for field in range(2):
        start(first_copy(field, 0, 0), 0)
    for field, side in both:
        wait_recv(edge_copy(field, side), side)
    first_level(0)
    first_level(cells - 1)
    for field, side in both:
        start(first_copy(field, side, 1), side)

    injection(1)
    planes(second_level, cells - H, cells - 1)
    for field in range(2):
        start(second_copy(0, field, 1, 0), 1)
    planes(second_level, 1, cells - H)
    for field in range(2):
        start(second_copy(0, field, 0, 0), 0)
    for field, side in both:
        wait_recv(first_copy(field, side, 1), side)
    second_level(0)
    second_level(cells - 1)
    for half in range(HALVES):
        for field, side in both:
            start(second_copy(half, field, side, 1), side)
    for field, side in both:
        start(second_copy(1, field, side, 0), side)

    def split(value, pieces):
        out = []
        for _ in range(pieces):
            out.append(value.astype(jnp.bfloat16))
            value = value - out[-1].astype(jnp.float32)
        return out

    def dot(one, other):
        return jnp.dot(one, other, preferred_element_type=jnp.float32)

    weight_load.wait()
    tall[...] = jnp.zeros(tall.shape, jnp.float32)
    for which in range(count):
        for a in range(3):
            for b in range(3):
                for c in range(3):
                    line = ((a * 3 + c) * 3 + b) * 16 + which
                    tall[line : line + 1] = conv_in[which, a, b, c : c + 1]
    line = 13 * 16 + count
    bias = bias_ref[...]
    tall[line : line + 1] = bias.astype(jnp.bfloat16).astype(jnp.float32)
    tall[line + 1 : line + 2] = bias - bias.astype(jnp.bfloat16).astype(jnp.float32)
    matrix_high, matrix_low = split(tall[...].T, 2)
    matrix_both = jnp.concatenate([matrix_high, matrix_low], axis=0)

    def products(level, rows_here, first):
        def body(which, carry):
            offset = offsets_ref[which]
            for block in range(coarse_x):
                total = None
                for inner in range(4):
                    x = H + block * 4 + inner
                    term = level[0, x + offset] * level[1, x - offset]
                    total = term if total is None else total + term
                if first:
                    acc[which, block] = total
                else:
                    acc[which, block, rows_here] = acc[which, block, rows_here] + total
            return carry

        lax.fori_loop(0, count, body, 0)

    lanes = coarse_x * coarse_z
    deep = coarse_x * size_z
    z_row = lax.broadcasted_iota(jnp.int32, (deep, lanes), 0)
    z_col = lax.broadcasted_iota(jnp.int32, (deep, lanes), 1)
    mean = jnp.where(jnp.right_shift(z_row, 2) == z_col, 1.0 / 64.0, 0.0).astype(jnp.bfloat16)
    rows[0] = jnp.zeros((count, lanes), jnp.float32)
    rows[coarse_y + 1] = jnp.zeros((count, lanes), jnp.float32)

    def means(half):
        wide = []
        for which in range(count):
            by_x = []
            for block in range(coarse_x):
                total = None
                for inner in range(4):
                    term = acc[which, block, pl.ds(half * half_y + inner, half_rows, stride=4)]
                    total = term if total is None else total + term
                by_x.append(total)
            wide.append(jnp.concatenate(by_x, axis=1))
        high = count * half_rows
        product = dot(jnp.concatenate(split(jnp.concatenate(wide, axis=0), 3), axis=0), mean)
        coarse = product[:high] + product[high : 2 * high] + product[2 * high :]
        for which in range(count):
            for y in range(half_rows):
                line = which * half_rows + y
                rows[1 + half * half_rows + y, which : which + 1] = coarse[line : line + 1]

    def row_copy(source, target):
        return remote(
            rows.at[pl.ds(target * own_rows, window)],
            parts.at[source],
            row_send.at[target],
            row_recv.at[source],
            {"shot": target},
        )

    def send_rows(targets):
        for target in targets:

            @pl.when(me_shot != target)
            def _():
                row_copy(me_shot, target).start()

    for field, side in both:
        wait_recv(first_copy(field, side, 0), side)
    products(first_lev, slice(0, size_y), True)
    sent = 0
    for half in range(HALVES):
        for field, side in both:
            wait_recv(second_copy(half, field, side, 1), side)
            wait_recv(second_copy(half, field, side, 0), side)
        products(second[half], slice(half * half_y, (half + 1) * half_y), False)
        means(half)
        done = shots if half == HALVES - 1 else ((half + 1) * half_rows + 1 - window) // own_rows + 1
        send_rows(range(sent, done))
        sent = done
    parts[me_shot] = rows[pl.ds(me_shot * own_rows, window)]
    total = None
    for source in range(shots):

        @pl.when(me_shot != source)
        def _():
            row_copy(source, source).wait_recv()

        total = parts[source] if total is None else total + parts[source]
    summed[1] = jnp.zeros(summed.shape[1:], jnp.float32)
    summed[1, :, 0:count] = total
    summed[1, :, count : count + 2] = jnp.ones((window, 2, lanes), jnp.float32)

    def rim_copy(side):
        return remote(
            summed.at[1],
            summed.at[(2, 0)[side]],
            rim_send.at[side],
            rim_recv.at[side],
            (left, right)[side],
        )

    for side in range(2):
        start(rim_copy(side), side)

    @pl.when(jnp.logical_not(has_left))
    def _():
        summed[0] = jnp.zeros(summed.shape[1:], jnp.float32)

    @pl.when(jnp.logical_not(has_right))
    def _():
        summed[2] = jnp.zeros(summed.shape[1:], jnp.float32)

    for side in range(2):
        wait_recv(rim_copy(side), side)

    flat = (window * 16, lanes)
    lane = lax.broadcasted_iota(jnp.int32, flat, 1)
    z_lane = jnp.bitwise_and(lane, coarse_z - 1)
    low, own, high = (summed[place].reshape(flat) for place in range(3))
    shifted = (
        jnp.where(lane < coarse_z, pltpu.roll(low, coarse_z, 1), pltpu.roll(own, coarse_z, 1)),
        own,
        jnp.where(
            lane >= lanes - coarse_z,
            pltpu.roll(high, lanes - coarse_z, 1),
            pltpu.roll(own, lanes - coarse_z, 1),
        ),
    )
    for a in range(3):
        patches[a * 3] = jnp.where(z_lane == 0, 0.0, pltpu.roll(shifted[a], 1, 1))
        patches[a * 3 + 1] = shifted[a]
        patches[a * 3 + 2] = jnp.where(
            z_lane == coarse_z - 1, 0.0, pltpu.roll(shifted[a], lanes - 1, 1)
        )
    columns = [
        jnp.concatenate([patches[k, y * 16 : y * 16 + 48] for k in range(9)], axis=0)
        for y in range(own_rows)
    ]
    columns_high, columns_low = split(jnp.concatenate(columns, axis=1), 2)
    channels = matrix_high.shape[0]
    product = dot(matrix_both, columns_high)
    product = product[:channels] + product[channels:] + dot(matrix_high, columns_low)
    for x in range(coarse_x):
        pieces = [
            product[:, y * lanes + x * coarse_z : y * lanes + (x + 1) * coarse_z]
            for y in range(own_rows)
        ]
        out_ref[pl.ds(x, channels, stride=coarse_x)] = jnp.concatenate(pieces, axis=1)

    for field, side in both:
        wait_send(edge_copy(field, side), side)
        for part in range(2):
            wait_send(first_copy(field, side, part), side)
            for half in range(HALVES):
                wait_send(second_copy(half, field, side, part), side)
    for target in range(shots):

        @pl.when(me_shot != target)
        def _():
            row_copy(me_shot, target).wait_send()

    for side in range(2):
        wait_send(rim_copy(side), side)


def local(
    source_prev,
    source_now,
    receiver_prev,
    receiver_now,
    courant,
    source_cells,
    wavelet,
    receiver_cells,
    receiver_data,
    offsets,
    conv_weight,
    conv_bias,
):
    cells, size_y, size_z = courant.shape
    shots, slabs = lax.axis_size("shot"), lax.axis_size("gx")
    count = offsets.shape[0]
    channels = conv_weight.shape[0]
    coarse_x, coarse_y, coarse_z = cells // 4, size_y // 4, size_z // 4
    own_rows = coarse_y // shots
    window = own_rows + 2
    lanes = coarse_x * coarse_z
    anywhere = pl.BlockSpec(memory_space=pltpu.HBM)
    vmem = pl.BlockSpec(memory_space=pltpu.VMEM)
    smem = pl.BlockSpec(memory_space=pltpu.SMEM)
    f32 = jnp.float32
    result = pl.pallas_call(
        functools.partial(kernel, (shots, slabs, cells, size_y, size_z, count)),
        out_shape=jax.ShapeDtypeStruct((channels * coarse_x, own_rows * coarse_z), f32),
        in_specs=[anywhere] * 5 + [vmem] * 4 + [smem, anywhere, vmem],
        out_specs=vmem,
        scratch_shapes=[
            pltpu.VMEM((2, cells + 2, size_y, size_z), f32),
            pltpu.VMEM((2, cells, size_y, size_z), f32),
            pltpu.VMEM((cells, size_y, size_z), f32),
            pltpu.VMEM((2, cells + 2 * HMAX, size_y, size_z), f32),
            pltpu.VMEM((2, cells + 2 * HMAX, size_y // HALVES, size_z), f32),
            pltpu.VMEM((2, cells + 2 * HMAX, size_y // HALVES, size_z), f32),
            pltpu.VMEM((2, 2, cells * size_y, size_z), f32),
            pltpu.VMEM((count, coarse_x, size_y, size_z), f32),
            pltpu.VMEM((8, 128), f32),
            pltpu.VMEM((8, 128), jnp.int32),
            pltpu.VMEM((coarse_y + 2, count, lanes), f32),
            pltpu.VMEM((shots, window, count, lanes), f32),
            pltpu.VMEM((3, window, 16, lanes), f32),
            pltpu.VMEM((9, window * 16, lanes), f32),
            pltpu.VMEM((count, 3, 3, 3, channels), f32),
            pltpu.VMEM((27 * 16, channels), f32),
            pltpu.SemaphoreType.DMA((6,)),
            pltpu.SemaphoreType.DMA((2, 2)),
            pltpu.SemaphoreType.DMA((2, 2)),
            pltpu.SemaphoreType.DMA((2, 2, 2)),
            pltpu.SemaphoreType.DMA((2, 2, 2)),
            pltpu.SemaphoreType.DMA((shots,)),
            pltpu.SemaphoreType.DMA((shots,)),
            pltpu.SemaphoreType.DMA((2,)),
            pltpu.SemaphoreType.DMA((2,)),
            pltpu.SemaphoreType.DMA((HALVES, 2, 2, 2)),
            pltpu.SemaphoreType.DMA((HALVES, 2, 2, 2)),
        ],
        compiler_params=pltpu.CompilerParams(
            collective_id=0, has_side_effects=True, vmem_limit_bytes=64 * 1024 * 1024 - 256 * 1024
        ),
        cost_estimate=pl.CostEstimate(
            flops=1_500_000_000, bytes_accessed=3_000_000, transcendentals=0
        ),
    )(
        source_prev,
        source_now,
        receiver_prev,
        receiver_now,
        courant,
        source_cells,
        wavelet,
        receiver_cells,
        receiver_data,
        offsets,
        conv_weight.transpose(1, 2, 3, 4, 0),
        conv_bias.reshape(1, channels),
    )
    return result.reshape(channels, coarse_x, own_rows * coarse_z)


def solution(mesh):
    in_specs = (
        P("shot", "gx", None, None),
        P("shot", "gx", None, None),
        P("shot", "gx", None, None),
        P("shot", "gx", None, None),
        P("gx", None, None),
        P("shot", None),
        P("shot", None, None),
        P("shot", None),
        P("shot", None, None),
        P(),
        P(),
        P(),
    )
    out_specs = P(None, "gx", "shot")
    return jax.shard_map(local, mesh=mesh, in_specs=in_specs, out_specs=out_specs, check_vma=False)
```

```python
import functools

import jax
import jax.numpy as jnp
from jax import lax
from jax.experimental import pallas as pl
from jax.experimental.pallas import tpu as pltpu
from jax.sharding import PartitionSpec as P

HMAX = 8
HALVES = 2
RIM = 2
MESH = pl.DeviceIdType.MESH


def kernel(
    dims,
    sp_ref,
    sn_ref,
    rp_ref,
    rn_ref,
    courant_ref,
    scells_ref,
    wavelet_ref,
    rcells_ref,
    rdata_ref,
    offsets_ref,
    weight_ref,
    bias_ref,
    out_ref,
    now,
    prev,
    cour,
    first_lev,
    second_low,
    second_high,
    inj,
    acc,
    pads,
    padi,
    rows,
    parts,
    summed,
    patches,
    conv_in,
    tall,
    load_sem,
    edge_send,
    edge_recv,
    lev_send,
    lev_recv,
    row_send,
    row_recv,
    rim_send,
    rim_recv,
    late_send,
    late_recv,
):
    shots, slabs, cells, size_y, size_z, count = dims
    me_shot = lax.axis_index("shot")
    me_gx = lax.axis_index("gx")
    has_left = me_gx > 0
    has_right = me_gx < slabs - 1
    left = {"gx": me_gx - 1}
    right = {"gx": me_gx + 1}
    coarse_x, coarse_y, coarse_z = cells // 4, size_y // 4, size_z // 4
    own_rows = coarse_y // shots
    window = own_rows + 2
    H = HMAX
    second = (second_low, second_high)
    half_y = size_y // HALVES
    half_rows = coarse_y // HALVES

    loads = [
        pltpu.make_async_copy(sn_ref.at[0], now.at[0, pl.ds(RIM, cells)], load_sem.at[0]),
        pltpu.make_async_copy(rn_ref.at[0], now.at[1, pl.ds(RIM, cells)], load_sem.at[1]),
        pltpu.make_async_copy(sp_ref.at[0], prev.at[0], load_sem.at[2]),
        pltpu.make_async_copy(rp_ref.at[0], prev.at[1], load_sem.at[3]),
        pltpu.make_async_copy(courant_ref, cour.at[pl.ds(RIM, cells)], load_sem.at[4]),
    ]
    for load in loads:
        load.start()
    weight_load = pltpu.make_async_copy(weight_ref, conv_in, load_sem.at[5])
    weight_load.start()

    barrier = pltpu.get_barrier_semaphore()
    for step in range(1, shots):
        pl.semaphore_signal(
            barrier,
            inc=1,
            device_id={"shot": lax.rem(me_shot + step, shots)},
            device_id_type=MESH,
        )

    @pl.when(has_left)
    def _():
        pl.semaphore_signal(barrier, inc=1, device_id=left, device_id_type=MESH)

    @pl.when(has_right)
    def _():
        pl.semaphore_signal(barrier, inc=1, device_id=right, device_id_type=MESH)

    pl.semaphore_wait(
        barrier, shots - 1 + has_left.astype(jnp.int32) + has_right.astype(jnp.int32)
    )

    def remote(src, dst, send, recv, target):
        return pltpu.make_async_remote_copy(
            src_ref=src,
            dst_ref=dst,
            send_sem=send,
            recv_sem=recv,
            device_id=target,
            device_id_type=MESH,
        )

    def edge_copy(kind, side):
        source = (sn_ref.at[0], rn_ref.at[0], courant_ref)[kind]
        target = (now.at[0], now.at[1], cour)[kind]
        plane, place = ((0, cells + RIM), (cells - RIM, 0))[side]
        return remote(
            source.at[pl.ds(plane, RIM)],
            target.at[pl.ds(place, RIM)],
            edge_send.at[kind, side],
            edge_recv.at[kind, side],
            (left, right)[side],
        )

    def place_of(side, part):
        if side == 0:
            first, size = ((1, H - 1), (0, 1))[part]
            return first, size, H + cells + first
        first, size = ((cells - H, H - 1), (cells - 1, 1))[part]
        return first, size, first - cells + H

    def first_copy(field, side, part):
        first, size, place = place_of(side, part)
        return remote(
            first_lev.at[field, pl.ds(H + first, size)],
            first_lev.at[field, pl.ds(place, size)],
            lev_send.at[field, side, part],
            lev_recv.at[field, side, part],
            (left, right)[side],
        )

    def second_copy(half, field, side):
        size = H - RIM
        first, place = ((RIM, H + cells + RIM), (cells - H, 0))[side]
        return remote(
            second[half].at[field, pl.ds(H + first, size)],
            second[half].at[field, pl.ds(place, size)],
            late_send.at[half, field, side],
            late_recv.at[half, field, side],
            (left, right)[side],
        )

    both = [(field, side) for field in range(2) for side in range(2)]
    edges = [(kind, side) for kind in range(3) for side in range(2)]

    def goes(side):
        return (has_left, has_right)[side]

    def comes(side):
        return (has_right, has_left)[side]

    def start(copy, side):
        @pl.when(goes(side))
        def _():
            copy.start()

    def wait_send(copy, side):
        @pl.when(goes(side))
        def _():
            copy.wait_send()

    def wait_recv(copy, side):
        @pl.when(comes(side))
        def _():
            copy.wait_recv()

    for kind, side in edges:
        start(edge_copy(kind, side), side)

    def clear(plane, place):
        for field in range(2):
            now[field, plane : plane + RIM] = jnp.zeros((RIM, size_y, size_z), jnp.float32)
            first_lev[field, place : place + H] = jnp.zeros((H, size_y, size_z), jnp.float32)
            for half in range(HALVES):
                second[half][field, place : place + H] = jnp.zeros(
                    (H, half_y, size_z), jnp.float32
                )

    @pl.when(jnp.logical_not(has_left))
    def _():
        clear(0, 0)

    @pl.when(jnp.logical_not(has_right))
    def _():
        clear(cells + RIM, H + cells)

    z_bits = size_z.bit_length() - 1
    first_row = me_gx * (cells * size_y)

    def spread(step, field, cell, amp):
        lanes = cell.shape[-1]
        z_of = jnp.bitwise_and(cell, size_z - 1)
        there = lax.broadcasted_iota(jnp.int32, (size_z, lanes), 0) == z_of
        high = amp.astype(jnp.bfloat16).astype(jnp.float32)
        pieces = [
            jnp.where(there, piece, 0.0).astype(jnp.bfloat16) for piece in (high, amp - high)
        ]
        right_side = jnp.concatenate(pieces, axis=0)
        extra = 0 if step == 0 else RIM
        count_x = cells + 2 * extra
        row_of = jnp.right_shift(cell, z_bits) - first_row + extra * size_y
        block = (8 if count_x % 8 == 0 else 4) * size_y

        def body(item, carry):
            first = item * block
            row = lax.broadcasted_iota(jnp.int32, (block, lanes), 0) + first
            hit = jnp.where(row == row_of, 1.0, 0.0).astype(jnp.bfloat16)
            value = lax.dot_general(
                hit, right_side, (((1,), (1,)), ((), ())), preferred_element_type=jnp.float32
            )
            at = pl.ds(pl.multiple_of(first, block), block)
            inj[step, field, at] = value[:, 0:size_z] + value[:, size_z:]
            return carry

        lax.fori_loop(0, count_x * size_y // block, body, 0, unroll=True)

    few = scells_ref.shape[-1]
    padi[...] = jnp.full(padi.shape, -1, jnp.int32)
    pads[...] = jnp.zeros(pads.shape, jnp.float32)
    padi[0:1, 0:few] = scells_ref[...]
    pads[0:2, 0:few] = wavelet_ref[0]

    def injection(step):
        spread(step, 0, padi[0:1], pads[step : step + 1])
        spread(step, 1, rcells_ref[...], rdata_ref[0, step : step + 1])

    injection(0)

    row_index = lax.broadcasted_iota(jnp.int32, (size_y, size_z), 0)
    lane_index = lax.broadcasted_iota(jnp.int32, (size_y, size_z), 1)

    def advance(before, low, center, high, speed, source):
        total = low + high
        total = total + jnp.where(row_index == 0, 0.0, pltpu.roll(center, 1, 0))
        total = total + jnp.where(row_index == size_y - 1, 0.0, pltpu.roll(center, size_y - 1, 0))
        total = total + jnp.where(lane_index == 0, 0.0, pltpu.roll(center, 1, 1))
        total = total + jnp.where(lane_index == size_z - 1, 0.0, pltpu.roll(center, size_z - 1, 1))
        return 2.0 * center - before + speed * (total - 6.0 * center) + source

    def first_level(x):
        speed = cour[RIM + x]
        for field in range(2):
            source = inj[0, field, pl.ds(pl.multiple_of(x * size_y, size_y), size_y)]
            first_lev[field, H + x] = advance(
                prev[field, x],
                now[field, RIM + x - 1],
                now[field, RIM + x],
                now[field, RIM + x + 1],
                speed,
                source,
            )

    def second_level(x):
        speed = cour[RIM + x]
        for field in range(2):
            line = pl.multiple_of((RIM + x) * size_y, size_y)
            source = inj[1, field, pl.ds(line, size_y)]
            value = advance(
                now[field, RIM + x],
                first_lev[field, H + x - 1],
                first_lev[field, H + x],
                first_lev[field, H + x + 1],
                speed,
                source,
            )
            for half in range(HALVES):
                second[half][field, H + x] = value[half * half_y : (half + 1) * half_y]

    def planes(one, first, last):
        def body(x, carry):
            one(x)
            return carry

        lax.fori_loop(first, last, body, 0, unroll=True)

    for load in loads:
        load.wait()
    planes(first_level, cells - H, cells - 1)
    for field in range(2):
        start(first_copy(field, 1, 0), 1)
    planes(first_level, 1, cells - H)
    for field in range(2):
        start(first_copy(field, 0, 0), 0)
    for field, side in both:
        wait_recv(edge_copy(field, side), side)
    first_level(0)
    first_level(cells - 1)
    for field, side in both:
        start(first_copy(field, side, 1), side)

    injection(1)
    planes(second_level, cells - H, cells - RIM)
    for half in range(HALVES):
        for field in range(2):
            start(second_copy(half, field, 1), 1)
    planes(second_level, RIM, cells - H)
    for half in range(HALVES):
        for field in range(2):
            start(second_copy(half, field, 0), 0)
    for field, side in both:
        wait_recv(first_copy(field, side, 1), side)
        wait_recv(first_copy(field, side, 0), side)
    for side in range(2):
        wait_recv(edge_copy(2, side), side)
    planes(second_level, 0, RIM)
    planes(second_level, cells - RIM, cells)

    @pl.when(has_left)
    def _():
        planes(second_level, -RIM, 0)

    @pl.when(has_right)
    def _():
        planes(second_level, cells, cells + RIM)

    def split(value, pieces):
        out = []
        for _ in range(pieces):
            out.append(value.astype(jnp.bfloat16))
            value = value - out[-1].astype(jnp.float32)
        return out

    def dot(one, other):
        return jnp.dot(one, other, preferred_element_type=jnp.float32)

    weight_load.wait()
    tall[...] = jnp.zeros(tall.shape, jnp.float32)
    for which in range(count):
        for a in range(3):
            for b in range(3):
                for c in range(3):
                    line = ((a * 3 + c) * 3 + b) * 16 + which
                    tall[line : line + 1] = conv_in[which, a, b, c : c + 1]
    line = 13 * 16 + count
    bias = bias_ref[...]
    tall[line : line + 1] = bias.astype(jnp.bfloat16).astype(jnp.float32)
    tall[line + 1 : line + 2] = bias - bias.astype(jnp.bfloat16).astype(jnp.float32)
    matrix_high, matrix_low = split(tall[...].T, 2)
    matrix_both = jnp.concatenate([matrix_high, matrix_low], axis=0)

    def products(level, rows_here, first):
        def body(which, carry):
            offset = offsets_ref[which]
            for block in range(coarse_x):
                total = None
                for inner in range(4):
                    x = H + block * 4 + inner
                    term = level[0, x + offset] * level[1, x - offset]
                    total = term if total is None else total + term
                if first:
                    acc[which, block] = total
                else:
                    acc[which, block, rows_here] = acc[which, block, rows_here] + total
            return carry

        lax.fori_loop(0, count, body, 0)

    lanes = coarse_x * coarse_z
    deep = coarse_x * size_z
    z_row = lax.broadcasted_iota(jnp.int32, (deep, lanes), 0)
    z_col = lax.broadcasted_iota(jnp.int32, (deep, lanes), 1)
    mean = jnp.where(jnp.right_shift(z_row, 2) == z_col, 1.0 / 64.0, 0.0).astype(jnp.bfloat16)
    rows[0] = jnp.zeros((count, lanes), jnp.float32)
    rows[coarse_y + 1] = jnp.zeros((count, lanes), jnp.float32)

    def means(half):
        wide = []
        for which in range(count):
            by_x = []
            for block in range(coarse_x):
                total = None
                for inner in range(4):
                    term = acc[which, block, pl.ds(half * half_y + inner, half_rows, stride=4)]
                    total = term if total is None else total + term
                by_x.append(total)
            wide.append(jnp.concatenate(by_x, axis=1))
        high = count * half_rows
        product = dot(jnp.concatenate(split(jnp.concatenate(wide, axis=0), 3), axis=0), mean)
        coarse = product[:high] + product[high : 2 * high] + product[2 * high :]
        for which in range(count):
            for y in range(half_rows):
                line = which * half_rows + y
                rows[1 + half * half_rows + y, which : which + 1] = coarse[line : line + 1]

    def row_copy(source, target):
        return remote(
            rows.at[pl.ds(target * own_rows, window)],
            parts.at[source],
            row_send.at[target],
            row_recv.at[source],
            {"shot": target},
        )

    def send_rows(targets):
        for target in targets:

            @pl.when(me_shot != target)
            def _():
                row_copy(me_shot, target).start()

    products(first_lev, slice(0, size_y), True)
    sent = 0
    for half in range(HALVES):
        for field, side in both:
            wait_recv(second_copy(half, field, side), side)
        products(second[half], slice(half * half_y, (half + 1) * half_y), False)
        means(half)
        done = shots if half == HALVES - 1 else ((half + 1) * half_rows + 1 - window) // own_rows + 1
        send_rows(range(sent, done))
        sent = done
    parts[me_shot] = rows[pl.ds(me_shot * own_rows, window)]
    total = None
    for source in range(shots):

        @pl.when(me_shot != source)
        def _():
            row_copy(source, source).wait_recv()

        total = parts[source] if total is None else total + parts[source]
    summed[1] = jnp.zeros(summed.shape[1:], jnp.float32)
    summed[1, :, 0:count] = total
    summed[1, :, count : count + 2] = jnp.ones((window, 2, lanes), jnp.float32)

    def rim_copy(side):
        return remote(
            summed.at[1],
            summed.at[(2, 0)[side]],
            rim_send.at[side],
            rim_recv.at[side],
            (left, right)[side],
        )

    for side in range(2):
        start(rim_copy(side), side)

    @pl.when(jnp.logical_not(has_left))
    def _():
        summed[0] = jnp.zeros(summed.shape[1:], jnp.float32)

    @pl.when(jnp.logical_not(has_right))
    def _():
        summed[2] = jnp.zeros(summed.shape[1:], jnp.float32)

    for side in range(2):
        wait_recv(rim_copy(side), side)

    flat = (window * 16, lanes)
    lane = lax.broadcasted_iota(jnp.int32, flat, 1)
    z_lane = jnp.bitwise_and(lane, coarse_z - 1)
    low, own, high = (summed[place].reshape(flat) for place in range(3))
    shifted = (
        jnp.where(lane < coarse_z, pltpu.roll(low, coarse_z, 1), pltpu.roll(own, coarse_z, 1)),
        own,
        jnp.where(
            lane >= lanes - coarse_z,
            pltpu.roll(high, lanes - coarse_z, 1),
            pltpu.roll(own, lanes - coarse_z, 1),
        ),
    )
    for a in range(3):
        patches[a * 3] = jnp.where(z_lane == 0, 0.0, pltpu.roll(shifted[a], 1, 1))
        patches[a * 3 + 1] = shifted[a]
        patches[a * 3 + 2] = jnp.where(
            z_lane == coarse_z - 1, 0.0, pltpu.roll(shifted[a], lanes - 1, 1)
        )
    columns = [
        jnp.concatenate([patches[k, y * 16 : y * 16 + 48] for k in range(9)], axis=0)
        for y in range(own_rows)
    ]
    columns_high, columns_low = split(jnp.concatenate(columns, axis=1), 2)
    channels = matrix_high.shape[0]
    product = dot(matrix_both, columns_high)
    product = product[:channels] + product[channels:] + dot(matrix_high, columns_low)
    for x in range(coarse_x):
        pieces = [
            product[:, y * lanes + x * coarse_z : y * lanes + (x + 1) * coarse_z]
            for y in range(own_rows)
        ]
        out_ref[pl.ds(x, channels, stride=coarse_x)] = jnp.concatenate(pieces, axis=1)

    for kind, side in edges:
        wait_send(edge_copy(kind, side), side)
    for field, side in both:
        for part in range(2):
            wait_send(first_copy(field, side, part), side)
        for half in range(HALVES):
            wait_send(second_copy(half, field, side), side)
    for target in range(shots):

        @pl.when(me_shot != target)
        def _():
            row_copy(me_shot, target).wait_send()

    for side in range(2):
        wait_send(rim_copy(side), side)


def local(
    source_prev,
    source_now,
    receiver_prev,
    receiver_now,
    courant,
    source_cells,
    wavelet,
    receiver_cells,
    receiver_data,
    offsets,
    conv_weight,
    conv_bias,
):
    cells, size_y, size_z = courant.shape
    shots, slabs = lax.axis_size("shot"), lax.axis_size("gx")
    count = offsets.shape[0]
    channels = conv_weight.shape[0]
    coarse_x, coarse_y, coarse_z = cells // 4, size_y // 4, size_z // 4
    own_rows = coarse_y // shots
    window = own_rows + 2
    lanes = coarse_x * coarse_z
    anywhere = pl.BlockSpec(memory_space=pltpu.HBM)
    vmem = pl.BlockSpec(memory_space=pltpu.VMEM)
    smem = pl.BlockSpec(memory_space=pltpu.SMEM)
    f32 = jnp.float32
    result = pl.pallas_call(
        functools.partial(kernel, (shots, slabs, cells, size_y, size_z, count)),
        out_shape=pltpu.VMEM((channels * coarse_x, own_rows * coarse_z), f32),
        in_specs=[anywhere] * 5 + [vmem] * 4 + [smem, anywhere, vmem],
        out_specs=vmem,
        scratch_shapes=[
            pltpu.VMEM((2, cells + 2 * RIM, size_y, size_z), f32),
            pltpu.VMEM((2, cells, size_y, size_z), f32),
            pltpu.VMEM((cells + 2 * RIM, size_y, size_z), f32),
            pltpu.VMEM((2, cells + 2 * HMAX, size_y, size_z), f32),
            pltpu.VMEM((2, cells + 2 * HMAX, size_y // HALVES, size_z), f32),
            pltpu.VMEM((2, cells + 2 * HMAX, size_y // HALVES, size_z), f32),
            pltpu.VMEM((2, 2, (cells + 2 * RIM) * size_y, size_z), f32),
            pltpu.VMEM((count, coarse_x, size_y, size_z), f32),
            pltpu.VMEM((8, 128), f32),
            pltpu.VMEM((8, 128), jnp.int32),
            pltpu.VMEM((coarse_y + 2, count, lanes), f32),
            pltpu.VMEM((shots, window, count, lanes), f32),
            pltpu.VMEM((3, window, 16, lanes), f32),
            pltpu.VMEM((9, window * 16, lanes), f32),
            pltpu.VMEM((count, 3, 3, 3, channels), f32),
            pltpu.VMEM((27 * 16, channels), f32),
            pltpu.SemaphoreType.DMA((6,)),
            pltpu.SemaphoreType.DMA((3, 2)),
            pltpu.SemaphoreType.DMA((3, 2)),
            pltpu.SemaphoreType.DMA((2, 2, 2)),
            pltpu.SemaphoreType.DMA((2, 2, 2)),
            pltpu.SemaphoreType.DMA((shots,)),
            pltpu.SemaphoreType.DMA((shots,)),
            pltpu.SemaphoreType.DMA((2,)),
            pltpu.SemaphoreType.DMA((2,)),
            pltpu.SemaphoreType.DMA((HALVES, 2, 2)),
            pltpu.SemaphoreType.DMA((HALVES, 2, 2)),
        ],
        compiler_params=pltpu.CompilerParams(
            collective_id=0, has_side_effects=True, vmem_limit_bytes=63 * 1024 * 1024
        ),
        cost_estimate=pl.CostEstimate(
            flops=1_500_000_000, bytes_accessed=3_000_000, transcendentals=0
        ),
    )(
        source_prev,
        source_now,
        receiver_prev,
        receiver_now,
        courant,
        source_cells,
        wavelet,
        receiver_cells,
        receiver_data,
        offsets,
        conv_weight.transpose(1, 2, 3, 4, 0),
        conv_bias.reshape(1, channels),
    )
    return result.reshape(channels, coarse_x, own_rows * coarse_z)


def solution(mesh):
    in_specs = (
        P("shot", "gx", None, None),
        P("shot", "gx", None, None),
        P("shot", "gx", None, None),
        P("shot", "gx", None, None),
        P("gx", None, None),
        P("shot", None),
        P("shot", None, None),
        P("shot", None),
        P("shot", None, None),
        P(),
        P(),
        P(),
    )
    out_specs = P(None, "gx", "shot")
    return jax.shard_map(local, mesh=mesh, in_specs=in_specs, out_specs=out_specs, check_vma=False)
```

```python
import functools

import jax
import jax.numpy as jnp
from jax import lax
from jax.experimental import pallas as pl
from jax.experimental.pallas import tpu as pltpu
from jax.sharding import PartitionSpec as P

HMAX = 8
PARTS = 4
RIM = 2
MESH = pl.DeviceIdType.MESH


def kernel(
    dims,
    sp_ref,
    sn_ref,
    rp_ref,
    rn_ref,
    courant_ref,
    scells_ref,
    wavelet_ref,
    rcells_ref,
    rdata_ref,
    offsets_ref,
    weight_ref,
    bias_ref,
    out_ref,
    now,
    prev,
    cour,
    first_lev,
    second_0,
    second_1,
    second_2,
    second_3,
    inj,
    acc,
    pads,
    padi,
    rows,
    parts,
    rim,
    summed,
    patches,
    conv_in,
    tall,
    load_sem,
    edge_send,
    edge_recv,
    lev_send,
    lev_recv,
    row_send,
    row_recv,
    rim_send,
    rim_recv,
    late_send,
    late_recv,
):
    shots, slabs, cells, size_y, size_z, count = dims
    me_shot = lax.axis_index("shot")
    me_gx = lax.axis_index("gx")
    has_left = me_gx > 0
    has_right = me_gx < slabs - 1
    left = {"gx": me_gx - 1}
    right = {"gx": me_gx + 1}
    coarse_x, coarse_y, coarse_z = cells // 4, size_y // 4, size_z // 4
    own_rows = coarse_y // shots
    window = own_rows + 2
    H = HMAX
    second = (second_0, second_1, second_2, second_3)
    half_y = size_y // PARTS
    half_rows = coarse_y // PARTS

    loads = [
        pltpu.make_async_copy(sn_ref.at[0], now.at[0, pl.ds(RIM, cells)], load_sem.at[0]),
        pltpu.make_async_copy(rn_ref.at[0], now.at[1, pl.ds(RIM, cells)], load_sem.at[1]),
        pltpu.make_async_copy(sp_ref.at[0], prev.at[0], load_sem.at[2]),
        pltpu.make_async_copy(rp_ref.at[0], prev.at[1], load_sem.at[3]),
        pltpu.make_async_copy(courant_ref, cour.at[pl.ds(RIM, cells)], load_sem.at[4]),
    ]
    for load in loads:
        load.start()
    weight_load = pltpu.make_async_copy(weight_ref, conv_in, load_sem.at[5])
    weight_load.start()

    barrier = pltpu.get_barrier_semaphore()
    for step in range(1, shots):
        pl.semaphore_signal(
            barrier,
            inc=1,
            device_id={"shot": lax.rem(me_shot + step, shots)},
            device_id_type=MESH,
        )

    @pl.when(has_left)
    def _():
        pl.semaphore_signal(barrier, inc=1, device_id=left, device_id_type=MESH)

    @pl.when(has_right)
    def _():
        pl.semaphore_signal(barrier, inc=1, device_id=right, device_id_type=MESH)

    has_up = me_shot > 0
    has_down = me_shot < shots - 1
    beside = [(dy, dx) for dy in (-1, 0, 1) for dx in (-1, 0, 1) if (dy, dx) != (0, 0)]

    def is_there(dy, dx):
        there_y = (has_up, None, has_down)[1 + dy]
        there_x = (has_left, None, has_right)[1 + dx]
        if there_y is None:
            return there_x
        return there_y if there_x is None else jnp.logical_and(there_y, there_x)

    def device_at(dy, dx):
        return {"shot": me_shot + dy, "gx": me_gx + dx}

    expected = shots - 1 + has_left.astype(jnp.int32) + has_right.astype(jnp.int32)
    for dy in (-1, 1):
        for dx in (-1, 1):
            expected = expected + is_there(dy, dx).astype(jnp.int32)

            @pl.when(is_there(dy, dx))
            def _():
                pl.semaphore_signal(
                    barrier, inc=1, device_id=device_at(dy, dx), device_id_type=MESH
                )

    pl.semaphore_wait(barrier, expected)

    def remote(src, dst, send, recv, target):
        return pltpu.make_async_remote_copy(
            src_ref=src,
            dst_ref=dst,
            send_sem=send,
            recv_sem=recv,
            device_id=target,
            device_id_type=MESH,
        )

    def edge_copy(kind, side):
        source = (sn_ref.at[0], rn_ref.at[0], courant_ref)[kind]
        target = (now.at[0], now.at[1], cour)[kind]
        plane, place = ((0, cells + RIM), (cells - RIM, 0))[side]
        return remote(
            source.at[pl.ds(plane, RIM)],
            target.at[pl.ds(place, RIM)],
            edge_send.at[kind, side],
            edge_recv.at[kind, side],
            (left, right)[side],
        )

    def place_of(side, part):
        if side == 0:
            first, size = ((1, H - 1), (0, 1))[part]
            return first, size, H + cells + first
        first, size = ((cells - H, H - 1), (cells - 1, 1))[part]
        return first, size, first - cells + H

    def first_copy(field, side, part):
        first, size, place = place_of(side, part)
        return remote(
            first_lev.at[field, pl.ds(H + first, size)],
            first_lev.at[field, pl.ds(place, size)],
            lev_send.at[field, side, part],
            lev_recv.at[field, side, part],
            (left, right)[side],
        )

    def second_copy(half, field, side):
        size = H - RIM
        first, place = ((RIM, H + cells + RIM), (cells - H, 0))[side]
        return remote(
            second[half].at[field, pl.ds(H + first, size)],
            second[half].at[field, pl.ds(place, size)],
            late_send.at[half, field, side],
            late_recv.at[half, field, side],
            (left, right)[side],
        )

    both = [(field, side) for field in range(2) for side in range(2)]
    edges = [(kind, side) for kind in range(3) for side in range(2)]

    def goes(side):
        return (has_left, has_right)[side]

    def comes(side):
        return (has_right, has_left)[side]

    def start(copy, side):
        @pl.when(goes(side))
        def _():
            copy.start()

    def wait_send(copy, side):
        @pl.when(goes(side))
        def _():
            copy.wait_send()

    def wait_recv(copy, side):
        @pl.when(comes(side))
        def _():
            copy.wait_recv()

    for kind, side in edges:
        start(edge_copy(kind, side), side)

    def clear(plane, place):
        for field in range(2):
            now[field, plane : plane + RIM] = jnp.zeros((RIM, size_y, size_z), jnp.float32)
            first_lev[field, place : place + H] = jnp.zeros((H, size_y, size_z), jnp.float32)
            for half in range(PARTS):
                second[half][field, place : place + H] = jnp.zeros(
                    (H, half_y, size_z), jnp.float32
                )

    @pl.when(jnp.logical_not(has_left))
    def _():
        clear(0, 0)

    @pl.when(jnp.logical_not(has_right))
    def _():
        clear(cells + RIM, H + cells)

    z_bits = size_z.bit_length() - 1
    first_row = me_gx * (cells * size_y)

    def spread(step, field, cell, amp):
        lanes = cell.shape[-1]
        z_of = jnp.bitwise_and(cell, size_z - 1)
        there = lax.broadcasted_iota(jnp.int32, (size_z, lanes), 0) == z_of
        high = amp.astype(jnp.bfloat16).astype(jnp.float32)
        pieces = [
            jnp.where(there, piece, 0.0).astype(jnp.bfloat16) for piece in (high, amp - high)
        ]
        right_side = jnp.concatenate(pieces, axis=0)
        extra = 0 if step == 0 else RIM
        count_x = cells + 2 * extra
        row_of = jnp.right_shift(cell, z_bits) - first_row + extra * size_y
        block = (8 if count_x % 8 == 0 else 4) * size_y

        def body(item, carry):
            first = item * block
            row = lax.broadcasted_iota(jnp.int32, (block, lanes), 0) + first
            hit = jnp.where(row == row_of, 1.0, 0.0).astype(jnp.bfloat16)
            value = lax.dot_general(
                hit, right_side, (((1,), (1,)), ((), ())), preferred_element_type=jnp.float32
            )
            at = pl.ds(pl.multiple_of(first, block), block)
            inj[step, field, at] = value[:, 0:size_z] + value[:, size_z:]
            return carry

        lax.fori_loop(0, count_x * size_y // block, body, 0, unroll=True)

    few = scells_ref.shape[-1]
    padi[...] = jnp.full(padi.shape, -1, jnp.int32)
    pads[...] = jnp.zeros(pads.shape, jnp.float32)
    padi[0:1, 0:few] = scells_ref[...]
    pads[0:2, 0:few] = wavelet_ref[0]

    def injection(step):
        spread(step, 0, padi[0:1], pads[step : step + 1])
        spread(step, 1, rcells_ref[...], rdata_ref[0, step : step + 1])

    injection(0)

    row_index = lax.broadcasted_iota(jnp.int32, (size_y, size_z), 0)
    lane_index = lax.broadcasted_iota(jnp.int32, (size_y, size_z), 1)

    def advance(before, low, center, high, speed, source):
        total = low + high
        total = total + jnp.where(row_index == 0, 0.0, pltpu.roll(center, 1, 0))
        total = total + jnp.where(row_index == size_y - 1, 0.0, pltpu.roll(center, size_y - 1, 0))
        total = total + jnp.where(lane_index == 0, 0.0, pltpu.roll(center, 1, 1))
        total = total + jnp.where(lane_index == size_z - 1, 0.0, pltpu.roll(center, size_z - 1, 1))
        return 2.0 * center - before + speed * (total - 6.0 * center) + source

    def first_level(x):
        speed = cour[RIM + x]
        for field in range(2):
            source = inj[0, field, pl.ds(pl.multiple_of(x * size_y, size_y), size_y)]
            first_lev[field, H + x] = advance(
                prev[field, x],
                now[field, RIM + x - 1],
                now[field, RIM + x],
                now[field, RIM + x + 1],
                speed,
                source,
            )

    def second_level(x):
        speed = cour[RIM + x]
        for field in range(2):
            line = pl.multiple_of((RIM + x) * size_y, size_y)
            source = inj[1, field, pl.ds(line, size_y)]
            value = advance(
                now[field, RIM + x],
                first_lev[field, H + x - 1],
                first_lev[field, H + x],
                first_lev[field, H + x + 1],
                speed,
                source,
            )
            for half in range(PARTS):
                second[half][field, H + x] = value[half * half_y : (half + 1) * half_y]

    def planes(one, first, last):
        def body(x, carry):
            one(x)
            return carry

        lax.fori_loop(first, last, body, 0, unroll=True)

    for load in loads:
        load.wait()
    planes(first_level, cells - H, cells - 1)
    for field in range(2):
        start(first_copy(field, 1, 0), 1)
    planes(first_level, 1, cells - H)
    for field in range(2):
        start(first_copy(field, 0, 0), 0)
    for field, side in both:
        wait_recv(edge_copy(field, side), side)
    first_level(0)
    first_level(cells - 1)
    for field, side in both:
        start(first_copy(field, side, 1), side)

    injection(1)
    planes(second_level, cells - H, cells - RIM)
    for half in range(PARTS):
        for field in range(2):
            start(second_copy(half, field, 1), 1)
    planes(second_level, RIM, cells - H)
    for half in range(PARTS):
        for field in range(2):
            start(second_copy(half, field, 0), 0)
    for field, side in both:
        wait_recv(first_copy(field, side, 1), side)
        wait_recv(first_copy(field, side, 0), side)
    for side in range(2):
        wait_recv(edge_copy(2, side), side)
    planes(second_level, 0, RIM)
    planes(second_level, cells - RIM, cells)

    @pl.when(has_left)
    def _():
        planes(second_level, -RIM, 0)

    @pl.when(has_right)
    def _():
        planes(second_level, cells, cells + RIM)

    def split(value, pieces):
        out = []
        for _ in range(pieces):
            out.append(value.astype(jnp.bfloat16))
            value = value - out[-1].astype(jnp.float32)
        return out

    def dot(one, other):
        return jnp.dot(one, other, preferred_element_type=jnp.float32)

    weight_load.wait()
    tall[...] = jnp.zeros(tall.shape, jnp.float32)
    for which in range(count):
        for a in range(3):
            for b in range(3):
                for c in range(3):
                    line = ((a * 3 + c) * 3 + b) * 16 + which
                    tall[line : line + 1] = conv_in[which, a, b, c : c + 1]
    line = 13 * 16 + count
    bias = bias_ref[...]
    tall[line : line + 1] = bias.astype(jnp.bfloat16).astype(jnp.float32)
    tall[line + 1 : line + 2] = bias - bias.astype(jnp.bfloat16).astype(jnp.float32)
    matrix_high, matrix_low = split(tall[...].T, 2)
    matrix_both = jnp.concatenate([matrix_high, matrix_low], axis=0)

    def products(level, rows_here, first):
        def body(which, carry):
            offset = offsets_ref[which]
            for block in range(coarse_x):
                total = None
                for inner in range(4):
                    x = H + block * 4 + inner
                    term = level[0, x + offset] * level[1, x - offset]
                    total = term if total is None else total + term
                if first:
                    acc[which, block] = total
                else:
                    acc[which, block, rows_here] = acc[which, block, rows_here] + total
            return carry

        lax.fori_loop(0, count, body, 0)

    lanes = coarse_x * coarse_z
    deep = coarse_x * size_z
    z_row = lax.broadcasted_iota(jnp.int32, (deep, lanes), 0)
    z_col = lax.broadcasted_iota(jnp.int32, (deep, lanes), 1)
    mean = jnp.where(jnp.right_shift(z_row, 2) == z_col, 1.0 / 64.0, 0.0).astype(jnp.bfloat16)
    summed[...] = jnp.zeros(summed.shape, jnp.float32)
    summed[1, :, count : count + 2] = jnp.ones((window, 2, lanes), jnp.float32)
    for dy, dx in beside:

        @pl.when(jnp.logical_not(is_there(dy, dx)))
        def _():
            rim[1 + dy, 1 + dx] = jnp.zeros(rim.shape[2:], jnp.float32)


    def means(half):
        wide = []
        for which in range(count):
            by_x = []
            for block in range(coarse_x):
                total = None
                for inner in range(4):
                    term = acc[which, block, pl.ds(half * half_y + inner, half_rows, stride=4)]
                    total = term if total is None else total + term
                by_x.append(total)
            wide.append(jnp.concatenate(by_x, axis=1))
        high = count * half_rows
        product = dot(jnp.concatenate(split(jnp.concatenate(wide, axis=0), 3), axis=0), mean)
        coarse = product[:high] + product[high : 2 * high] + product[2 * high :]
        for which in range(count):
            for y in range(half_rows):
                line = which * half_rows + y
                target, row = divmod(half * half_rows + y, own_rows)
                at = row * count + which
                rows[target, at : at + 1] = coarse[line : line + 1]

    def row_copy(source, target):
        return remote(
            rows.at[target],
            parts.at[source],
            row_send.at[target],
            row_recv.at[source],
            {"shot": target},
        )

    def send_rows(targets):
        for target in targets:

            @pl.when(me_shot != target)
            def _():
                row_copy(me_shot, target).start()

    products(first_lev, slice(0, size_y), True)
    sent = 0
    for half in range(PARTS):
        for field, side in both:
            wait_recv(second_copy(half, field, side), side)
        products(second[half], slice(half * half_y, (half + 1) * half_y), False)
        means(half)
        done = (half + 1) * half_rows // own_rows
        send_rows(range(sent, done))
        sent = done
    parts[me_shot] = rows[me_shot]
    total = None
    for source in range(shots):

        @pl.when(me_shot != source)
        def _():
            row_copy(source, source).wait_recv()

        total = parts[source] if total is None else total + parts[source]
    rim[1, 1] = total

    def rim_copy(dy, dx):
        return remote(
            rim.at[1, 1],
            rim.at[1 - dy, 1 - dx],
            rim_send.at[1 + dy, 1 + dx],
            rim_recv.at[1 - dy, 1 - dx],
            device_at(dy, dx),
        )

    for dy, dx in beside:

        @pl.when(is_there(dy, dx))
        def _():
            rim_copy(dy, dx).start()

    for dy, dx in beside:

        @pl.when(is_there(dy, dx))
        def _():
            rim_copy(-dy, -dx).wait_recv()

    for dx in range(3):
        summed[dx, 0, 0:count] = rim[0, dx, (own_rows - 1) * count : own_rows * count]
        for y in range(own_rows):
            summed[dx, 1 + y, 0:count] = rim[1, dx, y * count : (y + 1) * count]
        summed[dx, own_rows + 1, 0:count] = rim[2, dx, 0:count]

    flat = (window * 16, lanes)
    lane = lax.broadcasted_iota(jnp.int32, flat, 1)
    z_lane = jnp.bitwise_and(lane, coarse_z - 1)
    low, own, high = (summed[place].reshape(flat) for place in range(3))
    shifted = (
        jnp.where(lane < coarse_z, pltpu.roll(low, coarse_z, 1), pltpu.roll(own, coarse_z, 1)),
        own,
        jnp.where(
            lane >= lanes - coarse_z,
            pltpu.roll(high, lanes - coarse_z, 1),
            pltpu.roll(own, lanes - coarse_z, 1),
        ),
    )
    for a in range(3):
        patches[a * 3] = jnp.where(z_lane == 0, 0.0, pltpu.roll(shifted[a], 1, 1))
        patches[a * 3 + 1] = shifted[a]
        patches[a * 3 + 2] = jnp.where(
            z_lane == coarse_z - 1, 0.0, pltpu.roll(shifted[a], lanes - 1, 1)
        )
    columns = [
        jnp.concatenate([patches[k, y * 16 : y * 16 + 48] for k in range(9)], axis=0)
        for y in range(own_rows)
    ]
    columns_high, columns_low = split(jnp.concatenate(columns, axis=1), 2)
    channels = matrix_high.shape[0]
    product = dot(matrix_both, columns_high)
    product = product[:channels] + product[channels:] + dot(matrix_high, columns_low)
    for x in range(coarse_x):
        pieces = [
            product[:, y * lanes + x * coarse_z : y * lanes + (x + 1) * coarse_z]
            for y in range(own_rows)
        ]
        out_ref[pl.ds(x, channels, stride=coarse_x)] = jnp.concatenate(pieces, axis=1)

    for kind, side in edges:
        wait_send(edge_copy(kind, side), side)
    for field, side in both:
        for part in range(2):
            wait_send(first_copy(field, side, part), side)
        for half in range(PARTS):
            wait_send(second_copy(half, field, side), side)
    for target in range(shots):

        @pl.when(me_shot != target)
        def _():
            row_copy(me_shot, target).wait_send()

    for dy, dx in beside:

        @pl.when(is_there(dy, dx))
        def _():
            rim_copy(dy, dx).wait_send()


def local(
    source_prev,
    source_now,
    receiver_prev,
    receiver_now,
    courant,
    source_cells,
    wavelet,
    receiver_cells,
    receiver_data,
    offsets,
    conv_weight,
    conv_bias,
):
    cells, size_y, size_z = courant.shape
    shots, slabs = lax.axis_size("shot"), lax.axis_size("gx")
    count = offsets.shape[0]
    channels = conv_weight.shape[0]
    coarse_x, coarse_y, coarse_z = cells // 4, size_y // 4, size_z // 4
    own_rows = coarse_y // shots
    window = own_rows + 2
    lanes = coarse_x * coarse_z
    anywhere = pl.BlockSpec(memory_space=pltpu.HBM)
    vmem = pl.BlockSpec(memory_space=pltpu.VMEM)
    smem = pl.BlockSpec(memory_space=pltpu.SMEM)
    f32 = jnp.float32
    result = pl.pallas_call(
        functools.partial(kernel, (shots, slabs, cells, size_y, size_z, count)),
        out_shape=pltpu.VMEM((channels * coarse_x, own_rows * coarse_z), f32),
        in_specs=[anywhere] * 5 + [vmem] * 4 + [smem, anywhere, vmem],
        out_specs=vmem,
        scratch_shapes=[
            pltpu.VMEM((2, cells + 2 * RIM, size_y, size_z), f32),
            pltpu.VMEM((2, cells, size_y, size_z), f32),
            pltpu.VMEM((cells + 2 * RIM, size_y, size_z), f32),
            pltpu.VMEM((2, cells + 2 * HMAX, size_y, size_z), f32),
            pltpu.VMEM((2, cells + 2 * HMAX, size_y // PARTS, size_z), f32),
            pltpu.VMEM((2, cells + 2 * HMAX, size_y // PARTS, size_z), f32),
            pltpu.VMEM((2, cells + 2 * HMAX, size_y // PARTS, size_z), f32),
            pltpu.VMEM((2, cells + 2 * HMAX, size_y // PARTS, size_z), f32),
            pltpu.VMEM((2, 2, (cells + 2 * RIM) * size_y, size_z), f32),
            pltpu.VMEM((count, coarse_x, size_y, size_z), f32),
            pltpu.VMEM((8, 128), f32),
            pltpu.VMEM((8, 128), jnp.int32),
            pltpu.VMEM((shots, own_rows * count, lanes), f32),
            pltpu.VMEM((shots, own_rows * count, lanes), f32),
            pltpu.VMEM((3, 3, own_rows * count, lanes), f32),
            pltpu.VMEM((3, window, 16, lanes), f32),
            pltpu.VMEM((9, window * 16, lanes), f32),
            pltpu.VMEM((count, 3, 3, 3, channels), f32),
            pltpu.VMEM((27 * 16, channels), f32),
            pltpu.SemaphoreType.DMA((6,)),
            pltpu.SemaphoreType.DMA((3, 2)),
            pltpu.SemaphoreType.DMA((3, 2)),
            pltpu.SemaphoreType.DMA((2, 2, 2)),
            pltpu.SemaphoreType.DMA((2, 2, 2)),
            pltpu.SemaphoreType.DMA((shots,)),
            pltpu.SemaphoreType.DMA((shots,)),
            pltpu.SemaphoreType.DMA((3, 3)),
            pltpu.SemaphoreType.DMA((3, 3)),
            pltpu.SemaphoreType.DMA((PARTS, 2, 2)),
            pltpu.SemaphoreType.DMA((PARTS, 2, 2)),
        ],
        compiler_params=pltpu.CompilerParams(
            collective_id=0, has_side_effects=True, vmem_limit_bytes=63 * 1024 * 1024
        ),
        cost_estimate=pl.CostEstimate(
            flops=1_500_000_000, bytes_accessed=3_000_000, transcendentals=0
        ),
    )(
        source_prev,
        source_now,
        receiver_prev,
        receiver_now,
        courant,
        source_cells,
        wavelet,
        receiver_cells,
        receiver_data,
        offsets,
        conv_weight.transpose(1, 2, 3, 4, 0),
        conv_bias.reshape(1, channels),
    )
    return result.reshape(channels, coarse_x, own_rows * coarse_z)


def solution(mesh):
    in_specs = (
        P("shot", "gx", None, None),
        P("shot", "gx", None, None),
        P("shot", "gx", None, None),
        P("shot", "gx", None, None),
        P("gx", None, None),
        P("shot", None),
        P("shot", None, None),
        P("shot", None),
        P("shot", None, None),
        P(),
        P(),
        P(),
    )
    out_specs = P(None, "gx", "shot")
    return jax.shard_map(local, mesh=mesh, in_specs=in_specs, out_specs=out_specs, check_vma=False)
```

```python
import functools

import jax
import jax.numpy as jnp
from jax import lax
from jax.experimental import pallas as pl
from jax.experimental.pallas import tpu as pltpu
from jax.sharding import PartitionSpec as P

HMAX = 8
HALVES = 2
RIM = 2
MESH = pl.DeviceIdType.MESH


def kernel(
    dims,
    sp_ref,
    sn_ref,
    rp_ref,
    rn_ref,
    courant_ref,
    scells_ref,
    wavelet_ref,
    rcells_ref,
    rdata_ref,
    offsets_ref,
    weight_ref,
    bias_ref,
    out_ref,
    now,
    prev,
    cour,
    first_lev,
    second_low,
    second_high,
    inj,
    acc,
    pads,
    padi,
    rows,
    parts,
    summed,
    patches,
    conv_in,
    tall,
    load_sem,
    edge_send,
    edge_recv,
    lev_send,
    lev_recv,
    row_send,
    row_recv,
    rim_send,
    rim_recv,
    late_send,
    late_recv,
):
    shots, slabs, cells, size_y, size_z, count = dims
    me_shot = lax.axis_index("shot")
    me_gx = lax.axis_index("gx")
    has_left = me_gx > 0
    has_right = me_gx < slabs - 1
    left = {"gx": me_gx - 1}
    right = {"gx": me_gx + 1}
    coarse_x, coarse_y, coarse_z = cells // 4, size_y // 4, size_z // 4
    own_rows = coarse_y // shots
    window = own_rows + 2
    H = HMAX
    second = (second_low, second_high)
    half_y = size_y // HALVES
    half_rows = coarse_y // HALVES

    loads = [
        pltpu.make_async_copy(sn_ref.at[0], now.at[0, pl.ds(RIM, cells)], load_sem.at[0]),
        pltpu.make_async_copy(rn_ref.at[0], now.at[1, pl.ds(RIM, cells)], load_sem.at[1]),
        pltpu.make_async_copy(sp_ref.at[0], prev.at[0], load_sem.at[2]),
        pltpu.make_async_copy(rp_ref.at[0], prev.at[1], load_sem.at[3]),
        pltpu.make_async_copy(courant_ref, cour.at[pl.ds(RIM, cells)], load_sem.at[4]),
    ]
    for load in loads:
        load.start()
    weight_load = pltpu.make_async_copy(weight_ref, conv_in, load_sem.at[5])
    weight_load.start()

    barrier = pltpu.get_barrier_semaphore()
    for step in range(1, shots):
        pl.semaphore_signal(
            barrier,
            inc=1,
            device_id={"shot": lax.rem(me_shot + step, shots)},
            device_id_type=MESH,
        )

    @pl.when(has_left)
    def _():
        pl.semaphore_signal(barrier, inc=1, device_id=left, device_id_type=MESH)

    @pl.when(has_right)
    def _():
        pl.semaphore_signal(barrier, inc=1, device_id=right, device_id_type=MESH)

    pl.semaphore_wait(
        barrier, shots - 1 + has_left.astype(jnp.int32) + has_right.astype(jnp.int32)
    )

    def remote(src, dst, send, recv, target):
        return pltpu.make_async_remote_copy(
            src_ref=src,
            dst_ref=dst,
            send_sem=send,
            recv_sem=recv,
            device_id=target,
            device_id_type=MESH,
        )

    def edge_copy(kind, side):
        source = (sn_ref.at[0], rn_ref.at[0], courant_ref)[kind]
        target = (now.at[0], now.at[1], cour)[kind]
        plane, place = ((0, cells + RIM), (cells - RIM, 0))[side]
        return remote(
            source.at[pl.ds(plane, RIM)],
            target.at[pl.ds(place, RIM)],
            edge_send.at[kind, side],
            edge_recv.at[kind, side],
            (left, right)[side],
        )

    def place_of(side, part):
        if side == 0:
            first, size = ((1, H - 1), (0, 1))[part]
            return first, size, H + cells + first
        first, size = ((cells - H, H - 1), (cells - 1, 1))[part]
        return first, size, first - cells + H

    def first_copy(side, part):
        first, size, place = place_of(side, part)
        return remote(
            first_lev.at[:, pl.ds(H + first, size)],
            first_lev.at[:, pl.ds(place, size)],
            lev_send.at[side, part],
            lev_recv.at[side, part],
            (left, right)[side],
        )

    def second_copy(half, side):
        size = H - RIM
        first, place = ((RIM, H + cells + RIM), (cells - H, 0))[side]
        return remote(
            second[half].at[:, pl.ds(H + first, size)],
            second[half].at[:, pl.ds(place, size)],
            late_send.at[half, side],
            late_recv.at[half, side],
            (left, right)[side],
        )

    both = [(field, side) for field in range(2) for side in range(2)]
    edges = [(kind, side) for kind in range(3) for side in range(2)]

    def goes(side):
        return (has_left, has_right)[side]

    def comes(side):
        return (has_right, has_left)[side]

    def start(copy, side):
        @pl.when(goes(side))
        def _():
            copy.start()

    def wait_send(copy, side):
        @pl.when(goes(side))
        def _():
            copy.wait_send()

    def wait_recv(copy, side):
        @pl.when(comes(side))
        def _():
            copy.wait_recv()

    for kind, side in edges:
        start(edge_copy(kind, side), side)

    def clear(plane, place):
        for field in range(2):
            now[field, plane : plane + RIM] = jnp.zeros((RIM, size_y, size_z), jnp.float32)
            first_lev[field, place : place + H] = jnp.zeros((H, size_y, size_z), jnp.float32)
            for half in range(HALVES):
                second[half][field, place : place + H] = jnp.zeros(
                    (H, half_y, size_z), jnp.float32
                )

    @pl.when(jnp.logical_not(has_left))
    def _():
        clear(0, 0)

    @pl.when(jnp.logical_not(has_right))
    def _():
        clear(cells + RIM, H + cells)

    z_bits = size_z.bit_length() - 1
    first_row = me_gx * (cells * size_y)

    def spread(step, field, cell, amp):
        lanes = cell.shape[-1]
        z_of = jnp.bitwise_and(cell, size_z - 1)
        there = lax.broadcasted_iota(jnp.int32, (size_z, lanes), 0) == z_of
        high = amp.astype(jnp.bfloat16).astype(jnp.float32)
        pieces = [
            jnp.where(there, piece, 0.0).astype(jnp.bfloat16) for piece in (high, amp - high)
        ]
        right_side = jnp.concatenate(pieces, axis=0)
        extra = 0 if step == 0 else RIM
        count_x = cells + 2 * extra
        row_of = jnp.right_shift(cell, z_bits) - first_row + extra * size_y
        block = (8 if count_x % 8 == 0 else 4) * size_y

        def body(item, carry):
            first = item * block
            row = lax.broadcasted_iota(jnp.int32, (block, lanes), 0) + first
            hit = jnp.where(row == row_of, 1.0, 0.0).astype(jnp.bfloat16)
            value = lax.dot_general(
                hit, right_side, (((1,), (1,)), ((), ())), preferred_element_type=jnp.float32
            )
            at = pl.ds(pl.multiple_of(first, block), block)
            inj[step, field, at] = value[:, 0:size_z] + value[:, size_z:]
            return carry

        lax.fori_loop(0, count_x * size_y // block, body, 0, unroll=True)

    few = scells_ref.shape[-1]
    padi[...] = jnp.full(padi.shape, -1, jnp.int32)
    pads[...] = jnp.zeros(pads.shape, jnp.float32)
    padi[0:1, 0:few] = scells_ref[...]
    pads[0:2, 0:few] = wavelet_ref[0]

    def injection(step):
        spread(step, 0, padi[0:1], pads[step : step + 1])
        spread(step, 1, rcells_ref[...], rdata_ref[0, step : step + 1])

    injection(0)

    row_index = lax.broadcasted_iota(jnp.int32, (size_y, size_z), 0)
    lane_index = lax.broadcasted_iota(jnp.int32, (size_y, size_z), 1)

    def advance(before, low, center, high, speed, source):
        total = low + high
        total = total + jnp.where(row_index == 0, 0.0, pltpu.roll(center, 1, 0))
        total = total + jnp.where(row_index == size_y - 1, 0.0, pltpu.roll(center, size_y - 1, 0))
        total = total + jnp.where(lane_index == 0, 0.0, pltpu.roll(center, 1, 1))
        total = total + jnp.where(lane_index == size_z - 1, 0.0, pltpu.roll(center, size_z - 1, 1))
        return 2.0 * center - before + speed * (total - 6.0 * center) + source

    def first_level(x):
        speed = cour[RIM + x]
        for field in range(2):
            source = inj[0, field, pl.ds(pl.multiple_of(x * size_y, size_y), size_y)]
            first_lev[field, H + x] = advance(
                prev[field, x],
                now[field, RIM + x - 1],
                now[field, RIM + x],
                now[field, RIM + x + 1],
                speed,
                source,
            )

    def second_level(x):
        speed = cour[RIM + x]
        for field in range(2):
            line = pl.multiple_of((RIM + x) * size_y, size_y)
            source = inj[1, field, pl.ds(line, size_y)]
            value = advance(
                now[field, RIM + x],
                first_lev[field, H + x - 1],
                first_lev[field, H + x],
                first_lev[field, H + x + 1],
                speed,
                source,
            )
            for half in range(HALVES):
                second[half][field, H + x] = value[half * half_y : (half + 1) * half_y]

    def planes(one, first, last):
        def body(x, carry):
            one(x)
            return carry

        lax.fori_loop(first, last, body, 0, unroll=True)

    for load in loads:
        load.wait()
    planes(first_level, cells - H, cells - 1)
    start(first_copy(1, 0), 1)
    planes(first_level, 1, cells - H)
    start(first_copy(0, 0), 0)
    for field, side in both:
        wait_recv(edge_copy(field, side), side)
    first_level(0)
    first_level(cells - 1)
    for side in range(2):
        start(first_copy(side, 1), side)

    injection(1)
    planes(second_level, cells - H, cells - RIM)
    for half in range(HALVES):
        start(second_copy(half, 1), 1)
    planes(second_level, RIM, cells - H)
    for half in range(HALVES):
        start(second_copy(half, 0), 0)
    def split(value, pieces):
        out = []
        for _ in range(pieces):
            out.append(value.astype(jnp.bfloat16))
            value = value - out[-1].astype(jnp.float32)
        return out

    def dot(one, other):
        return jnp.dot(one, other, preferred_element_type=jnp.float32)

    weight_load.wait()
    tall[...] = jnp.zeros(tall.shape, jnp.float32)
    for which in range(count):
        for a in range(3):
            for b in range(3):
                line = (a * 9 + b) * 16 + which
                tall[pl.ds(line, 3, stride=48)] = conv_in[which, a, b]
    line = 13 * 16 + count
    bias = bias_ref[...]
    tall[line : line + 1] = bias.astype(jnp.bfloat16).astype(jnp.float32)
    tall[line + 1 : line + 2] = bias - bias.astype(jnp.bfloat16).astype(jnp.float32)
    matrix_high, matrix_low = split(tall[...].T, 2)
    matrix_both = jnp.concatenate([matrix_high, matrix_low], axis=0)

    lanes = coarse_x * coarse_z
    summed[1] = jnp.zeros(summed.shape[1:], jnp.float32)
    summed[1, :, count : count + 2] = jnp.ones((window, 2, lanes), jnp.float32)

    @pl.when(jnp.logical_not(has_left))
    def _():
        summed[0] = jnp.zeros(summed.shape[1:], jnp.float32)

    @pl.when(jnp.logical_not(has_right))
    def _():
        summed[2] = jnp.zeros(summed.shape[1:], jnp.float32)

    for side in range(2):
        wait_recv(first_copy(side, 1), side)
    planes(second_level, 0, RIM)
    planes(second_level, cells - RIM, cells)
    for side in range(2):
        wait_recv(first_copy(side, 0), side)
        wait_recv(edge_copy(2, side), side)

    @pl.when(has_left)
    def _():
        planes(second_level, -RIM, 0)

    @pl.when(has_right)
    def _():
        planes(second_level, cells, cells + RIM)

    def products(level, rows_here, first):
        def body(which, carry):
            offset = offsets_ref[which]
            for block in range(coarse_x):
                total = None
                for inner in range(4):
                    x = H + block * 4 + inner
                    term = level[0, x + offset] * level[1, x - offset]
                    total = term if total is None else total + term
                if first:
                    acc[which, block] = total
                else:
                    acc[which, block, rows_here] = acc[which, block, rows_here] + total
            return carry

        lax.fori_loop(0, count, body, 0)

    deep = coarse_x * size_z
    z_row = lax.broadcasted_iota(jnp.int32, (deep, lanes), 0)
    z_col = lax.broadcasted_iota(jnp.int32, (deep, lanes), 1)
    mean = jnp.where(jnp.right_shift(z_row, 2) == z_col, 1.0 / 64.0, 0.0).astype(jnp.bfloat16)
    rows[0] = jnp.zeros((count, lanes), jnp.float32)
    rows[coarse_y + 1] = jnp.zeros((count, lanes), jnp.float32)

    def means(half):
        wide = []
        for which in range(count):
            by_x = []
            for block in range(coarse_x):
                total = None
                for inner in range(4):
                    term = acc[which, block, pl.ds(half * half_y + inner, half_rows, stride=4)]
                    total = term if total is None else total + term
                by_x.append(total)
            wide.append(jnp.concatenate(by_x, axis=1))
        high = count * half_rows
        product = dot(jnp.concatenate(split(jnp.concatenate(wide, axis=0), 3), axis=0), mean)
        coarse = product[:high] + product[high : 2 * high] + product[2 * high :]
        for which in range(count):
            for y in range(half_rows):
                line = which * half_rows + y
                rows[1 + half * half_rows + y, which : which + 1] = coarse[line : line + 1]

    def row_copy(source, target):
        return remote(
            rows.at[pl.ds(target * own_rows, window)],
            parts.at[source],
            row_send.at[target],
            row_recv.at[source],
            {"shot": target},
        )

    def send_rows(targets):
        for target in targets:

            @pl.when(me_shot != target)
            def _():
                row_copy(me_shot, target).start()

    products(first_lev, slice(0, size_y), True)
    for kind, side in edges:
        wait_send(edge_copy(kind, side), side)
    for side in range(2):
        for part in range(2):
            wait_send(first_copy(side, part), side)
    sent = 0
    for half in range(HALVES):
        for side in range(2):
            wait_recv(second_copy(half, side), side)
        products(second[half], slice(half * half_y, (half + 1) * half_y), False)
        means(half)
        done = shots if half == HALVES - 1 else ((half + 1) * half_rows + 1 - window) // own_rows + 1
        send_rows(range(sent, done))
        sent = done
    for half in range(HALVES):
        for side in range(2):
            wait_send(second_copy(half, side), side)
    parts[me_shot] = rows[pl.ds(me_shot * own_rows, window)]
    total = None
    for source in range(shots):

        @pl.when(me_shot != source)
        def _():
            row_copy(source, source).wait_recv()

        total = parts[source] if total is None else total + parts[source]
    summed[1, :, 0:count] = total

    def rim_copy(side):
        return remote(
            summed.at[1],
            summed.at[(2, 0)[side]],
            rim_send.at[side],
            rim_recv.at[side],
            (left, right)[side],
        )

    for side in range(2):
        start(rim_copy(side), side)
    for target in range(shots):

        @pl.when(me_shot != target)
        def _():
            row_copy(me_shot, target).wait_send()

    for side in range(2):
        wait_recv(rim_copy(side), side)

    flat = (window * 16, lanes)
    lane = lax.broadcasted_iota(jnp.int32, flat, 1)
    z_lane = jnp.bitwise_and(lane, coarse_z - 1)
    low, own, high = (summed[place].reshape(flat) for place in range(3))
    shifted = (
        jnp.where(lane < coarse_z, pltpu.roll(low, coarse_z, 1), pltpu.roll(own, coarse_z, 1)),
        own,
        jnp.where(
            lane >= lanes - coarse_z,
            pltpu.roll(high, lanes - coarse_z, 1),
            pltpu.roll(own, lanes - coarse_z, 1),
        ),
    )
    for a in range(3):
        patches[a * 3] = jnp.where(z_lane == 0, 0.0, pltpu.roll(shifted[a], 1, 1))
        patches[a * 3 + 1] = shifted[a]
        patches[a * 3 + 2] = jnp.where(
            z_lane == coarse_z - 1, 0.0, pltpu.roll(shifted[a], lanes - 1, 1)
        )
    columns = [
        jnp.concatenate([patches[k, y * 16 : y * 16 + 48] for k in range(9)], axis=0)
        for y in range(own_rows)
    ]
    columns_high, columns_low = split(jnp.concatenate(columns, axis=1), 2)
    channels = matrix_high.shape[0]
    product = dot(matrix_both, columns_high)
    product = product[:channels] + product[channels:] + dot(matrix_high, columns_low)
    for x in range(coarse_x):
        pieces = [
            product[:, y * lanes + x * coarse_z : y * lanes + (x + 1) * coarse_z]
            for y in range(own_rows)
        ]
        out_ref[pl.ds(x, channels, stride=coarse_x)] = jnp.concatenate(pieces, axis=1)

    for side in range(2):
        wait_send(rim_copy(side), side)


def local(
    source_prev,
    source_now,
    receiver_prev,
    receiver_now,
    courant,
    source_cells,
    wavelet,
    receiver_cells,
    receiver_data,
    offsets,
    conv_weight,
    conv_bias,
):
    cells, size_y, size_z = courant.shape
    shots, slabs = lax.axis_size("shot"), lax.axis_size("gx")
    count = offsets.shape[0]
    channels = conv_weight.shape[0]
    coarse_x, coarse_y, coarse_z = cells // 4, size_y // 4, size_z // 4
    own_rows = coarse_y // shots
    window = own_rows + 2
    lanes = coarse_x * coarse_z
    anywhere = pl.BlockSpec(memory_space=pltpu.HBM)
    vmem = pl.BlockSpec(memory_space=pltpu.VMEM)
    smem = pl.BlockSpec(memory_space=pltpu.SMEM)
    f32 = jnp.float32
    result = pl.pallas_call(
        functools.partial(kernel, (shots, slabs, cells, size_y, size_z, count)),
        out_shape=pltpu.VMEM((channels * coarse_x, own_rows * coarse_z), f32),
        in_specs=[anywhere] * 5 + [vmem] * 4 + [smem, anywhere, vmem],
        out_specs=vmem,
        scratch_shapes=[
            pltpu.VMEM((2, cells + 2 * RIM, size_y, size_z), f32),
            pltpu.VMEM((2, cells, size_y, size_z), f32),
            pltpu.VMEM((cells + 2 * RIM, size_y, size_z), f32),
            pltpu.VMEM((2, cells + 2 * HMAX, size_y, size_z), f32),
            pltpu.VMEM((2, cells + 2 * HMAX, size_y // HALVES, size_z), f32),
            pltpu.VMEM((2, cells + 2 * HMAX, size_y // HALVES, size_z), f32),
            pltpu.VMEM((2, 2, (cells + 2 * RIM) * size_y, size_z), f32),
            pltpu.VMEM((count, coarse_x, size_y, size_z), f32),
            pltpu.VMEM((8, 128), f32),
            pltpu.VMEM((8, 128), jnp.int32),
            pltpu.VMEM((coarse_y + 2, count, lanes), f32),
            pltpu.VMEM((shots, window, count, lanes), f32),
            pltpu.VMEM((3, window, 16, lanes), f32),
            pltpu.VMEM((9, window * 16, lanes), f32),
            pltpu.VMEM((count, 3, 3, 3, channels), f32),
            pltpu.VMEM((27 * 16, channels), f32),
            pltpu.SemaphoreType.DMA((6,)),
            pltpu.SemaphoreType.DMA((3, 2)),
            pltpu.SemaphoreType.DMA((3, 2)),
            pltpu.SemaphoreType.DMA((2, 2)),
            pltpu.SemaphoreType.DMA((2, 2)),
            pltpu.SemaphoreType.DMA((shots,)),
            pltpu.SemaphoreType.DMA((shots,)),
            pltpu.SemaphoreType.DMA((2,)),
            pltpu.SemaphoreType.DMA((2,)),
            pltpu.SemaphoreType.DMA((HALVES, 2)),
            pltpu.SemaphoreType.DMA((HALVES, 2)),
        ],
        compiler_params=pltpu.CompilerParams(
            collective_id=0, has_side_effects=True, vmem_limit_bytes=63 * 1024 * 1024
        ),
        cost_estimate=pl.CostEstimate(
            flops=1_500_000_000, bytes_accessed=3_000_000, transcendentals=0
        ),
    )(
        source_prev,
        source_now,
        receiver_prev,
        receiver_now,
        courant,
        source_cells,
        wavelet,
        receiver_cells,
        receiver_data,
        offsets,
        conv_weight.transpose(1, 2, 3, 4, 0),
        conv_bias.reshape(1, channels),
    )
    return result.reshape(channels, coarse_x, own_rows * coarse_z)


def solution(mesh):
    in_specs = (
        P("shot", "gx", None, None),
        P("shot", "gx", None, None),
        P("shot", "gx", None, None),
        P("shot", "gx", None, None),
        P("gx", None, None),
        P("shot", None),
        P("shot", None, None),
        P("shot", None),
        P("shot", None, None),
        P(),
        P(),
        P(),
    )
    out_specs = P(None, "gx", "shot")
    return jax.shard_map(local, mesh=mesh, in_specs=in_specs, out_specs=out_specs, check_vma=False)
```

```python
import functools

import jax
import jax.numpy as jnp
from jax import lax
from jax.experimental import pallas as pl
from jax.experimental.pallas import tpu as pltpu
from jax.sharding import PartitionSpec as P

HMAX = 8
HALVES = 2
RIM = 2
MESH = pl.DeviceIdType.MESH


def kernel(
    dims,
    sp_ref,
    sn_ref,
    rp_ref,
    rn_ref,
    courant_ref,
    scells_ref,
    wavelet_ref,
    rcells_ref,
    rdata_ref,
    offsets_ref,
    weight_ref,
    bias_ref,
    out_ref,
    now,
    prev,
    cour,
    first_lev,
    second_low,
    second_high,
    inj,
    acc,
    pads,
    padi,
    rows,
    parts,
    summed,
    patches,
    conv_in,
    tall,
    load_sem,
    edge_send,
    edge_recv,
    lev_send,
    lev_recv,
    row_send,
    row_recv,
    rim_send,
    rim_recv,
    late_send,
    late_recv,
):
    shots, slabs, cells, size_y, size_z, count = dims
    me_shot = lax.axis_index("shot")
    me_gx = lax.axis_index("gx")
    has_left = me_gx > 0
    has_right = me_gx < slabs - 1
    left = {"gx": me_gx - 1}
    right = {"gx": me_gx + 1}
    coarse_x, coarse_y, coarse_z = cells // 4, size_y // 4, size_z // 4
    own_rows = coarse_y // shots
    window = own_rows + 2
    H = HMAX
    second = (second_low, second_high)
    half_y = size_y // HALVES
    half_rows = coarse_y // HALVES

    loads = [
        pltpu.make_async_copy(sn_ref.at[0], now.at[0, pl.ds(RIM, cells)], load_sem.at[0]),
        pltpu.make_async_copy(rn_ref.at[0], now.at[1, pl.ds(RIM, cells)], load_sem.at[1]),
        pltpu.make_async_copy(sp_ref.at[0], prev.at[0], load_sem.at[2]),
        pltpu.make_async_copy(rp_ref.at[0], prev.at[1], load_sem.at[3]),
        pltpu.make_async_copy(courant_ref, cour.at[pl.ds(RIM, cells)], load_sem.at[4]),
    ]
    for load in loads:
        load.start()
    weight_load = pltpu.make_async_copy(weight_ref, conv_in, load_sem.at[5])
    weight_load.start()

    barrier = pltpu.get_barrier_semaphore()
    for step in range(1, shots):
        pl.semaphore_signal(
            barrier,
            inc=1,
            device_id={"shot": lax.rem(me_shot + step, shots)},
            device_id_type=MESH,
        )

    @pl.when(has_left)
    def _():
        pl.semaphore_signal(barrier, inc=1, device_id=left, device_id_type=MESH)

    @pl.when(has_right)
    def _():
        pl.semaphore_signal(barrier, inc=1, device_id=right, device_id_type=MESH)

    pl.semaphore_wait(
        barrier, shots - 1 + has_left.astype(jnp.int32) + has_right.astype(jnp.int32)
    )

    def remote(src, dst, send, recv, target):
        return pltpu.make_async_remote_copy(
            src_ref=src,
            dst_ref=dst,
            send_sem=send,
            recv_sem=recv,
            device_id=target,
            device_id_type=MESH,
        )

    def edge_copy(kind, side):
        source = (sn_ref.at[0], rn_ref.at[0], courant_ref)[kind]
        target = (now.at[0], now.at[1], cour)[kind]
        plane, place = ((0, cells + RIM), (cells - RIM, 0))[side]
        return remote(
            source.at[pl.ds(plane, RIM)],
            target.at[pl.ds(place, RIM)],
            edge_send.at[kind, side],
            edge_recv.at[kind, side],
            (left, right)[side],
        )

    def place_of(side, part):
        if side == 0:
            first, size = ((1, H - 1), (0, 1))[part]
            return first, size, H + cells + first
        first, size = ((cells - H, H - 1), (cells - 1, 1))[part]
        return first, size, first - cells + H

    def first_copy(side, part):
        first, size, place = place_of(side, part)
        return remote(
            first_lev.at[:, pl.ds(H + first, size)],
            first_lev.at[:, pl.ds(place, size)],
            lev_send.at[side, part],
            lev_recv.at[side, part],
            (left, right)[side],
        )

    def second_copy(half, side):
        size = H - RIM
        first, place = ((RIM, H + cells + RIM), (cells - H, 0))[side]
        return remote(
            second[half].at[:, pl.ds(H + first, size)],
            second[half].at[:, pl.ds(place, size)],
            late_send.at[half, side],
            late_recv.at[half, side],
            (left, right)[side],
        )

    both = [(field, side) for field in range(2) for side in range(2)]
    edges = [(kind, side) for kind in range(3) for side in range(2)]

    def goes(side):
        return (has_left, has_right)[side]

    def comes(side):
        return (has_right, has_left)[side]

    def start(copy, side):
        @pl.when(goes(side))
        def _():
            copy.start()

    def wait_send(copy, side):
        @pl.when(goes(side))
        def _():
            copy.wait_send()

    def wait_recv(copy, side):
        @pl.when(comes(side))
        def _():
            copy.wait_recv()

    for kind, side in edges:
        start(edge_copy(kind, side), side)

    def clear(plane, place):
        for field in range(2):
            now[field, plane : plane + RIM] = jnp.zeros((RIM, size_y, size_z), jnp.float32)
            first_lev[field, place : place + H] = jnp.zeros((H, size_y, size_z), jnp.float32)
            for half in range(HALVES):
                second[half][field, place : place + H] = jnp.zeros(
                    (H, half_y, size_z), jnp.float32
                )

    @pl.when(jnp.logical_not(has_left))
    def _():
        clear(0, 0)

    @pl.when(jnp.logical_not(has_right))
    def _():
        clear(cells + RIM, H + cells)

    z_bits = size_z.bit_length() - 1
    first_row = me_gx * (cells * size_y)

    def spread(step, field, cell, amp):
        lanes = cell.shape[-1]
        z_of = jnp.bitwise_and(cell, size_z - 1)
        there = lax.broadcasted_iota(jnp.int32, (size_z, lanes), 0) == z_of
        high = amp.astype(jnp.bfloat16).astype(jnp.float32)
        pieces = [
            jnp.where(there, piece, 0.0).astype(jnp.bfloat16) for piece in (high, amp - high)
        ]
        right_side = jnp.concatenate(pieces, axis=0)
        extra = 0 if step == 0 else RIM
        count_x = cells + 2 * extra
        row_of = jnp.right_shift(cell, z_bits) - first_row + extra * size_y
        block = (8 if count_x % 8 == 0 else 4) * size_y

        def body(item, carry):
            first = item * block
            row = lax.broadcasted_iota(jnp.int32, (block, lanes), 0) + first
            hit = jnp.where(row == row_of, 1.0, 0.0).astype(jnp.bfloat16)
            value = lax.dot_general(
                hit, right_side, (((1,), (1,)), ((), ())), preferred_element_type=jnp.float32
            )
            at = pl.ds(pl.multiple_of(first, block), block)
            inj[step, field, at] = value[:, 0:size_z] + value[:, size_z:]
            return carry

        lax.fori_loop(0, count_x * size_y // block, body, 0, unroll=True)

    few = scells_ref.shape[-1]
    padi[...] = jnp.full(padi.shape, -1, jnp.int32)
    pads[...] = jnp.zeros(pads.shape, jnp.float32)
    padi[0:1, 0:few] = scells_ref[...]
    pads[0:2, 0:few] = wavelet_ref[0]

    def injection(step):
        spread(step, 0, padi[0:1], pads[step : step + 1])
        spread(step, 1, rcells_ref[...], rdata_ref[0, step : step + 1])

    injection(0)

    row_index = lax.broadcasted_iota(jnp.int32, (size_y, size_z), 0)
    lane_index = lax.broadcasted_iota(jnp.int32, (size_y, size_z), 1)

    def advance(before, low, center, high, speed, source):
        total = low + high
        total = total + jnp.where(row_index == 0, 0.0, pltpu.roll(center, 1, 0))
        total = total + jnp.where(row_index == size_y - 1, 0.0, pltpu.roll(center, size_y - 1, 0))
        total = total + jnp.where(lane_index == 0, 0.0, pltpu.roll(center, 1, 1))
        total = total + jnp.where(lane_index == size_z - 1, 0.0, pltpu.roll(center, size_z - 1, 1))
        return 2.0 * center - before + speed * (total - 6.0 * center) + source

    def first_level(x):
        speed = cour[RIM + x]
        for field in range(2):
            source = inj[0, field, pl.ds(pl.multiple_of(x * size_y, size_y), size_y)]
            first_lev[field, H + x] = advance(
                prev[field, x],
                now[field, RIM + x - 1],
                now[field, RIM + x],
                now[field, RIM + x + 1],
                speed,
                source,
            )

    def second_level(x):
        speed = cour[RIM + x]
        for field in range(2):
            line = pl.multiple_of((RIM + x) * size_y, size_y)
            source = inj[1, field, pl.ds(line, size_y)]
            value = advance(
                now[field, RIM + x],
                first_lev[field, H + x - 1],
                first_lev[field, H + x],
                first_lev[field, H + x + 1],
                speed,
                source,
            )
            for half in range(HALVES):
                second[half][field, H + x] = value[half * half_y : (half + 1) * half_y]

    def planes(one, first, last):
        def body(x, carry):
            one(x)
            return carry

        lax.fori_loop(first, last, body, 0, unroll=True)

    far_right = me_gx % 2 == 1

    def sides_in_order(one, first_plane, size, copies):
        for turn in range(2):
            to_right = far_right if turn == 0 else jnp.logical_not(far_right)
            base = jnp.where(to_right, first_plane[1], first_plane[0])
            planes(lambda x: one(base + x), 0, size)
            for side in range(2):
                here = to_right if side == 1 else jnp.logical_not(to_right)

                @pl.when(jnp.logical_and(here, goes(side)))
                def _():
                    for copy in copies(side):
                        copy.start()

    for load in loads:
        load.wait()
    sides_in_order(first_level, (1, cells - H), H - 1, lambda side: [first_copy(side, 0)])
    for field, side in both:
        wait_recv(edge_copy(field, side), side)
    first_level(0)
    first_level(cells - 1)
    for side in range(2):
        start(first_copy(side, 1), side)

    injection(1)
    sides_in_order(
        second_level,
        (RIM, cells - H),
        H - RIM,
        lambda side: [second_copy(half, side) for half in range(HALVES)],
    )
    def split(value, pieces):
        out = []
        for _ in range(pieces):
            out.append(value.astype(jnp.bfloat16))
            value = value - out[-1].astype(jnp.float32)
        return out

    def dot(one, other):
        return jnp.dot(one, other, preferred_element_type=jnp.float32)

    weight_load.wait()
    tall[...] = jnp.zeros(tall.shape, jnp.float32)
    for which in range(count):
        for a in range(3):
            for b in range(3):
                line = (a * 9 + b) * 16 + which
                tall[pl.ds(line, 3, stride=48)] = conv_in[which, a, b]
    line = 13 * 16 + count
    bias = bias_ref[...]
    tall[line : line + 1] = bias.astype(jnp.bfloat16).astype(jnp.float32)
    tall[line + 1 : line + 2] = bias - bias.astype(jnp.bfloat16).astype(jnp.float32)
    matrix_high, matrix_low = split(tall[...].T, 2)
    matrix_both = jnp.concatenate([matrix_high, matrix_low], axis=0)

    lanes = coarse_x * coarse_z
    summed[1] = jnp.zeros(summed.shape[1:], jnp.float32)
    summed[1, :, count : count + 2] = jnp.ones((window, 2, lanes), jnp.float32)

    @pl.when(jnp.logical_not(has_left))
    def _():
        summed[0] = jnp.zeros(summed.shape[1:], jnp.float32)

    @pl.when(jnp.logical_not(has_right))
    def _():
        summed[2] = jnp.zeros(summed.shape[1:], jnp.float32)

    for side in range(2):
        wait_recv(first_copy(side, 1), side)
    planes(second_level, 0, RIM)
    planes(second_level, cells - RIM, cells)
    for side in range(2):
        wait_recv(first_copy(side, 0), side)
        wait_recv(edge_copy(2, side), side)

    @pl.when(has_left)
    def _():
        planes(second_level, -RIM, 0)

    @pl.when(has_right)
    def _():
        planes(second_level, cells, cells + RIM)

    def products(level, rows_here, first):
        def body(which, carry):
            offset = offsets_ref[which]
            for block in range(coarse_x):
                total = None
                for inner in range(4):
                    x = H + block * 4 + inner
                    term = level[0, x + offset] * level[1, x - offset]
                    total = term if total is None else total + term
                if first:
                    acc[which, block] = total
                else:
                    acc[which, block, rows_here] = acc[which, block, rows_here] + total
            return carry

        lax.fori_loop(0, count, body, 0)

    deep = coarse_x * size_z
    z_row = lax.broadcasted_iota(jnp.int32, (deep, lanes), 0)
    z_col = lax.broadcasted_iota(jnp.int32, (deep, lanes), 1)
    mean = jnp.where(jnp.right_shift(z_row, 2) == z_col, 1.0 / 64.0, 0.0).astype(jnp.bfloat16)
    rows[0] = jnp.zeros((count, lanes), jnp.float32)
    rows[coarse_y + 1] = jnp.zeros((count, lanes), jnp.float32)

    def means(half):
        wide = []
        for which in range(count):
            by_x = []
            for block in range(coarse_x):
                total = None
                for inner in range(4):
                    term = acc[which, block, pl.ds(half * half_y + inner, half_rows, stride=4)]
                    total = term if total is None else total + term
                by_x.append(total)
            wide.append(jnp.concatenate(by_x, axis=1))
        high = count * half_rows
        product = dot(jnp.concatenate(split(jnp.concatenate(wide, axis=0), 3), axis=0), mean)
        coarse = product[:high] + product[high : 2 * high] + product[2 * high :]
        for which in range(count):
            for y in range(half_rows):
                line = which * half_rows + y
                rows[1 + half * half_rows + y, which : which + 1] = coarse[line : line + 1]

    def row_copy(source, target):
        return remote(
            rows.at[pl.ds(target * own_rows, window)],
            parts.at[source],
            row_send.at[target],
            row_recv.at[source],
            {"shot": target},
        )

    def send_rows(targets):
        for target in targets:

            @pl.when(me_shot != target)
            def _():
                row_copy(me_shot, target).start()

    products(first_lev, slice(0, size_y), True)
    for kind, side in edges:
        wait_send(edge_copy(kind, side), side)
    for side in range(2):
        for part in range(2):
            wait_send(first_copy(side, part), side)
    sent = 0
    for half in range(HALVES):
        for side in range(2):
            wait_recv(second_copy(half, side), side)
        products(second[half], slice(half * half_y, (half + 1) * half_y), False)
        means(half)
        done = shots if half == HALVES - 1 else ((half + 1) * half_rows + 1 - window) // own_rows + 1
        send_rows(range(sent, done))
        sent = done
    for half in range(HALVES):
        for side in range(2):
            wait_send(second_copy(half, side), side)
    parts[me_shot] = rows[pl.ds(me_shot * own_rows, window)]
    total = None
    for source in range(shots):

        @pl.when(me_shot != source)
        def _():
            row_copy(source, source).wait_recv()

        total = parts[source] if total is None else total + parts[source]
    summed[1, :, 0:count] = total

    def rim_copy(side):
        return remote(
            summed.at[1],
            summed.at[(2, 0)[side]],
            rim_send.at[side],
            rim_recv.at[side],
            (left, right)[side],
        )

    for side in range(2):
        start(rim_copy(side), side)
    for target in range(shots):

        @pl.when(me_shot != target)
        def _():
            row_copy(me_shot, target).wait_send()

    for side in range(2):
        wait_recv(rim_copy(side), side)

    flat = (window * 16, lanes)
    lane = lax.broadcasted_iota(jnp.int32, flat, 1)
    z_lane = jnp.bitwise_and(lane, coarse_z - 1)
    low, own, high = (summed[place].reshape(flat) for place in range(3))
    shifted = (
        jnp.where(lane < coarse_z, pltpu.roll(low, coarse_z, 1), pltpu.roll(own, coarse_z, 1)),
        own,
        jnp.where(
            lane >= lanes - coarse_z,
            pltpu.roll(high, lanes - coarse_z, 1),
            pltpu.roll(own, lanes - coarse_z, 1),
        ),
    )
    for a in range(3):
        patches[a * 3] = jnp.where(z_lane == 0, 0.0, pltpu.roll(shifted[a], 1, 1))
        patches[a * 3 + 1] = shifted[a]
        patches[a * 3 + 2] = jnp.where(
            z_lane == coarse_z - 1, 0.0, pltpu.roll(shifted[a], lanes - 1, 1)
        )
    columns = [
        jnp.concatenate([patches[k, y * 16 : y * 16 + 48] for k in range(9)], axis=0)
        for y in range(own_rows)
    ]
    columns_high, columns_low = split(jnp.concatenate(columns, axis=1), 2)
    channels = matrix_high.shape[0]
    product = dot(matrix_both, columns_high)
    product = product[:channels] + product[channels:] + dot(matrix_high, columns_low)
    for x in range(coarse_x):
        pieces = [
            product[:, y * lanes + x * coarse_z : y * lanes + (x + 1) * coarse_z]
            for y in range(own_rows)
        ]
        out_ref[pl.ds(x, channels, stride=coarse_x)] = jnp.concatenate(pieces, axis=1)

    for side in range(2):
        wait_send(rim_copy(side), side)


def local(
    source_prev,
    source_now,
    receiver_prev,
    receiver_now,
    courant,
    source_cells,
    wavelet,
    receiver_cells,
    receiver_data,
    offsets,
    conv_weight,
    conv_bias,
):
    cells, size_y, size_z = courant.shape
    shots, slabs = lax.axis_size("shot"), lax.axis_size("gx")
    count = offsets.shape[0]
    channels = conv_weight.shape[0]
    coarse_x, coarse_y, coarse_z = cells // 4, size_y // 4, size_z // 4
    own_rows = coarse_y // shots
    window = own_rows + 2
    lanes = coarse_x * coarse_z
    anywhere = pl.BlockSpec(memory_space=pltpu.HBM)
    vmem = pl.BlockSpec(memory_space=pltpu.VMEM)
    smem = pl.BlockSpec(memory_space=pltpu.SMEM)
    f32 = jnp.float32
    result = pl.pallas_call(
        functools.partial(kernel, (shots, slabs, cells, size_y, size_z, count)),
        out_shape=pltpu.VMEM((channels * coarse_x, own_rows * coarse_z), f32),
        in_specs=[anywhere] * 5 + [vmem] * 4 + [smem, anywhere, vmem],
        out_specs=vmem,
        scratch_shapes=[
            pltpu.VMEM((2, cells + 2 * RIM, size_y, size_z), f32),
            pltpu.VMEM((2, cells, size_y, size_z), f32),
            pltpu.VMEM((cells + 2 * RIM, size_y, size_z), f32),
            pltpu.VMEM((2, cells + 2 * HMAX, size_y, size_z), f32),
            pltpu.VMEM((2, cells + 2 * HMAX, size_y // HALVES, size_z), f32),
            pltpu.VMEM((2, cells + 2 * HMAX, size_y // HALVES, size_z), f32),
            pltpu.VMEM((2, 2, (cells + 2 * RIM) * size_y, size_z), f32),
            pltpu.VMEM((count, coarse_x, size_y, size_z), f32),
            pltpu.VMEM((8, 128), f32),
            pltpu.VMEM((8, 128), jnp.int32),
            pltpu.VMEM((coarse_y + 2, count, lanes), f32),
            pltpu.VMEM((shots, window, count, lanes), f32),
            pltpu.VMEM((3, window, 16, lanes), f32),
            pltpu.VMEM((9, window * 16, lanes), f32),
            pltpu.VMEM((count, 3, 3, 3, channels), f32),
            pltpu.VMEM((27 * 16, channels), f32),
            pltpu.SemaphoreType.DMA((6,)),
            pltpu.SemaphoreType.DMA((3, 2)),
            pltpu.SemaphoreType.DMA((3, 2)),
            pltpu.SemaphoreType.DMA((2, 2)),
            pltpu.SemaphoreType.DMA((2, 2)),
            pltpu.SemaphoreType.DMA((shots,)),
            pltpu.SemaphoreType.DMA((shots,)),
            pltpu.SemaphoreType.DMA((2,)),
            pltpu.SemaphoreType.DMA((2,)),
            pltpu.SemaphoreType.DMA((HALVES, 2)),
            pltpu.SemaphoreType.DMA((HALVES, 2)),
        ],
        compiler_params=pltpu.CompilerParams(
            collective_id=0, has_side_effects=True, vmem_limit_bytes=63 * 1024 * 1024
        ),
        cost_estimate=pl.CostEstimate(
            flops=1_500_000_000, bytes_accessed=3_000_000, transcendentals=0
        ),
    )(
        source_prev,
        source_now,
        receiver_prev,
        receiver_now,
        courant,
        source_cells,
        wavelet,
        receiver_cells,
        receiver_data,
        offsets,
        conv_weight.transpose(1, 2, 3, 4, 0),
        conv_bias.reshape(1, channels),
    )
    return result.reshape(channels, coarse_x, own_rows * coarse_z)


def solution(mesh):
    in_specs = (
        P("shot", "gx", None, None),
        P("shot", "gx", None, None),
        P("shot", "gx", None, None),
        P("shot", "gx", None, None),
        P("gx", None, None),
        P("shot", None),
        P("shot", None, None),
        P("shot", None),
        P("shot", None, None),
        P(),
        P(),
        P(),
    )
    out_specs = P(None, "gx", "shot")
    return jax.shard_map(local, mesh=mesh, in_specs=in_specs, out_specs=out_specs, check_vma=False)
```
